256 devices in a mesh: row: 32 (over z, y_lo, core), col: 8 (over x, y_hi).
Axes of the slice: x: 4, y: 4 (y_hi: 2, y_lo: 2; y = y_hi * 2 + y_lo), z: 8, core: 2. Of those that a mesh axis runs over, the one named last changes fastest.
Arguments:
- pair: bfloat16 [512, 512, 128], P('row', 'col'), may hold values from -6 to 6
- input_norm_gain: float32 [128], replicated, may hold values from 0.1 to 1.9
- input_norm_bias: float32 [128], replicated, may hold values from -3 to 3
- frozen_base_weight: float32 [128, 512], replicated, may hold values from -0.5 to 0.5
- adapter_down_factor: float32 [128, 16], replicated, may hold values from -0.6 to 0.6
- adapter_up_factor: float32 [16, 512], replicated, may hold values from -1.5 to 1.5
- magnitude: float32 [512], replicated, may hold values from 0.5 to 2
- output_gate_weight: bfloat16 [128, 128], replicated, may hold values from -0.5 to 0.5
- output_projection_weight: bfloat16 [128, 128], replicated, may hold values from -0.5 to 0.5
- centre_norm_gain: float32 [128], replicated, may hold values from 0.1 to 1.9
- centre_norm_bias: float32 [128], replicated, may hold values from -3 to 3
- cotangent: bfloat16 [512, 512, 128], P('row', 'col'), may hold values from -6 to 6
Outputs:
- update: bfloat16 [512, 512, 128], P('row', 'col')
- pair_input_gradient: bfloat16 [512, 512, 128], P('row', 'col')
- down_factor_gradient: float32 [128, 16], replicated
- up_factor_gradient: float32 [16, 512], replicated
- magnitude_vector_gradient: float32 [512], replicated
The draws below stay inside these ranges and needn't reach their ends.
All inputs are finite; a program needn't handle non-finite values.
Results may differ from the reference program's by a relative error of at most 0.02.
Values may be sent and summed in bfloat16 or wider, within the bound.
A program may use at most 128 MiB of HBM per device.

```python
import math
import jax
import jax.numpy as jnp
from jax import lax

PAIR_CHANNELS = 128
ADAPTER_RANK = 16
RB = 16
N = 512


def block_levels(key, shape, cuts, least, top_value):
    loudness = 1.0
    for dim, shards_of in cuts:
        draws = jax.random.uniform(jax.random.fold_in(jax.random.fold_in(key, 6), dim), (shards_of,), jnp.float32, least / len(cuts), top_value / len(cuts))
        loudness = loudness * jnp.repeat(jnp.exp(draws), shape[dim] // shards_of).reshape((-1,) + (1,) * (len(shape) - 1 - dim))
    return loudness


def normal_values(rng, dims, spread, reach, cuts=(), kind=jnp.bfloat16):
    loudness = block_levels(rng, dims, cuts, -0.22, 0.18) if cuts else 1.0
    entries = jax.random.normal(rng, dims, jnp.float32) * spread * loudness
    return jnp.minimum(jnp.maximum(entries, -reach), reach).astype(kind)


def setup_inputs(seed: int = 0) -> dict:
    splits = jax.random.split(jax.random.key(seed), 13)
    pair = normal_values(splits[0], (N, N, PAIR_CHANNELS), 1.0, 6.0, ((0, 32), (1, 8)))
    input_norm_gain = jnp.clip(1.0 + 0.18 * jax.random.normal(splits[1], (PAIR_CHANNELS,), jnp.float32), 0.1, 1.9)
    input_norm_bias = normal_values(splits[2], (PAIR_CHANNELS,), 0.5, 3.0, (), jnp.float32)
    frozen_base_weight = normal_values(splits[3], (PAIR_CHANNELS, 4 * PAIR_CHANNELS), PAIR_CHANNELS ** -0.5, 0.5, (), jnp.float32)
    adapter_down_factor = normal_values(splits[4], (PAIR_CHANNELS, ADAPTER_RANK), 0.1, 0.6, (), jnp.float32)
    adapter_up_factor = normal_values(splits[5], (ADAPTER_RANK, 4 * PAIR_CHANNELS), ADAPTER_RANK ** -0.5, 1.5, (), jnp.float32)
    magnitude = jnp.clip(jnp.exp(jax.random.uniform(splits[6], (4 * PAIR_CHANNELS,), jnp.float32, math.log(0.5), math.log(2.0))), 0.5, 2.0)
    output_gate_weight = normal_values(splits[7], (PAIR_CHANNELS, PAIR_CHANNELS), PAIR_CHANNELS ** -0.5, 0.5)
    output_projection_weight = normal_values(splits[8], (PAIR_CHANNELS, PAIR_CHANNELS), PAIR_CHANNELS ** -0.5, 0.5)
    centre_norm_gain = jnp.clip(1.0 + 0.18 * jax.random.normal(splits[9], (PAIR_CHANNELS,), jnp.float32), 0.1, 1.9)
    centre_norm_bias = normal_values(splits[10], (PAIR_CHANNELS,), 0.5, 3.0, (), jnp.float32)
    cotangent = normal_values(splits[11], (N, N, PAIR_CHANNELS), 1.0, 6.0, ((0, 32), (1, 8)))
    return dict(pair=pair, input_norm_gain=input_norm_gain, input_norm_bias=input_norm_bias, frozen_base_weight=frozen_base_weight, adapter_down_factor=adapter_down_factor, adapter_up_factor=adapter_up_factor, magnitude=magnitude, output_gate_weight=output_gate_weight, output_projection_weight=output_projection_weight, centre_norm_gain=centre_norm_gain, centre_norm_bias=centre_norm_bias, cotangent=cotangent)


def norm_parts(v):
    mean = lax.optimization_barrier(jnp.mean(v, axis=-1, keepdims=True))
    centred = v - mean
    inv = lax.rsqrt(lax.optimization_barrier(jnp.mean(centred * centred, axis=-1, keepdims=True)) + 1e-05)
    return (centred * inv, inv)

def norm_back(grad_hat, zhat, inv):
    return inv * (grad_hat - lax.optimization_barrier(jnp.mean(grad_hat, -1, keepdims=True)) - zhat * lax.optimization_barrier(jnp.mean(grad_hat * zhat, -1, keepdims=True)))

def reference(pair, input_norm_gain, input_norm_bias, frozen_base_weight, adapter_down_factor, adapter_up_factor, magnitude, output_gate_weight, output_projection_weight, centre_norm_gain, centre_norm_bias, cotangent):
    single_float = jnp.float32
    highest_precision = lax.Precision.HIGHEST
    zhat1, inv1 = norm_parts(pair.astype(single_float))
    zb = (zhat1 * input_norm_gain + input_norm_bias).astype(jnp.bfloat16)
    direction_matrix = frozen_base_weight + jnp.dot(adapter_down_factor, adapter_up_factor, precision=highest_precision, preferred_element_type=single_float)
    column_norm = jnp.sqrt(lax.optimization_barrier(jnp.sum(direction_matrix * direction_matrix, axis=0)) + 1e-06)
    adapter_scale = magnitude / column_norm
    merged_weight_matrix = (direction_matrix * adapter_scale).astype(jnp.bfloat16)
    cells = zb.reshape(-1, PAIR_CHANNELS)
    proj = jnp.dot(cells, merged_weight_matrix, preferred_element_type=single_float).reshape(N, N, 4 * PAIR_CHANNELS)
    sig_a = jax.nn.sigmoid(proj[..., 0:PAIR_CHANNELS])
    val_a = proj[..., PAIR_CHANNELS:2 * PAIR_CHANNELS]
    sig_b = jax.nn.sigmoid(proj[..., 2 * PAIR_CHANNELS:3 * PAIR_CHANNELS])
    val_b = proj[..., 3 * PAIR_CHANNELS:4 * PAIR_CHANNELS]
    left = (sig_a * val_a).astype(jnp.bfloat16)
    right = (sig_b * val_b).astype(jnp.bfloat16)
    left_f = left.astype(single_float)
    right_f = right.astype(single_float)
    xsum = jnp.einsum('ikc,jkc->ijc', left_f, right_f)
    zhat2, inv2 = norm_parts(xsum)
    xb = (zhat2 * centre_norm_gain + centre_norm_bias).astype(jnp.bfloat16)
    gate = jax.nn.sigmoid(jnp.dot(cells, output_gate_weight, preferred_element_type=single_float)).reshape(N, N, PAIR_CHANNELS)
    outp = jnp.dot(xb.reshape(-1, PAIR_CHANNELS), output_projection_weight, preferred_element_type=single_float).reshape(N, N, PAIR_CHANNELS)
    update = (gate * outp).astype(jnp.bfloat16)
    cot = cotangent.astype(single_float)
    egrad = (cot * gate).astype(jnp.bfloat16)
    dgp = (cot * outp * gate * (1.0 - gate)).astype(jnp.bfloat16)
    dxn = jnp.dot(egrad.reshape(-1, PAIR_CHANNELS), output_projection_weight.T, preferred_element_type=single_float).reshape(N, N, PAIR_CHANNELS)
    dxb = norm_back(dxn * centre_norm_gain, zhat2, inv2).astype(jnp.bfloat16)
    dxf = dxb.astype(single_float)
    dleft = jnp.einsum('ijc,jkc->ikc', dxf, right_f)

    def block_step(total, index):
        start = (index * RB).astype(jnp.int32)
        blk_dx = lax.dynamic_slice_in_dim(dxf, start, RB, 0)
        blk_a = lax.dynamic_slice_in_dim(left_f, start, RB, 0)
        part = jnp.einsum('ijc,ikc->jkc', blk_dx, blk_a)
        part = lax.optimization_barrier(part.astype(jnp.bfloat16)).astype(single_float)
        return (total + part, None)
    dright, _ = lax.scan(block_step, jnp.zeros((N, N, PAIR_CHANNELS), single_float), jnp.arange(N // RB, dtype=jnp.int32))
    dproj = jnp.concatenate([dleft * val_a * sig_a * (1.0 - sig_a), dleft * sig_a, dright * val_b * sig_b * (1.0 - sig_b), dright * sig_b], axis=-1).astype(jnp.bfloat16)
    dproj_cells = dproj.reshape(-1, 4 * PAIR_CHANNELS)
    dzb = jnp.dot(dproj_cells, merged_weight_matrix.T, preferred_element_type=single_float) + jnp.dot(dgp.reshape(-1, PAIR_CHANNELS), output_gate_weight.T, preferred_element_type=single_float)
    pair_input_gradient = norm_back(dzb.reshape(N, N, PAIR_CHANNELS) * input_norm_gain, zhat1, inv1).astype(jnp.bfloat16)
    merged_weight_gradient = jnp.dot(cells.T, dproj_cells, preferred_element_type=single_float) / N
    device_reduce_sum = lax.optimization_barrier(jnp.sum(merged_weight_gradient * direction_matrix, axis=0))
    magnitude_vector_gradient = device_reduce_sum / column_norm
    direction_gradient = merged_weight_gradient * adapter_scale - direction_matrix * (magnitude * device_reduce_sum / (column_norm * column_norm * column_norm))
    down_factor_gradient = jnp.dot(direction_gradient, adapter_up_factor.T, precision=highest_precision, preferred_element_type=single_float)
    up_factor_gradient = jnp.dot(adapter_down_factor.T, direction_gradient, precision=highest_precision, preferred_element_type=single_float)
    return (update, pair_input_gradient, down_factor_gradient, up_factor_gradient, magnitude_vector_gradient)
```

```python
import jax
import jax.numpy as jnp
from jax import lax
from jax.experimental import pallas as pl
from jax.experimental.pallas import tpu as pltpu
from jax.sharding import PartitionSpec as P

MESH = pl.DeviceIdType.MESH
F32 = jnp.float32
BF16 = jnp.bfloat16
NZ, NY, NX = 8, 4, 4
CH = 128
TOKENS = 512
HIGHEST = lax.Precision.HIGHEST


def dot(a, b, ca=1, cb=0, precision=None):
    return lax.dot_general(
        a, b, (((ca,), (cb,)), ((), ())), precision=precision, preferred_element_type=F32
    )


def far_first(k, n):
    return n // 2 + (1 - 2 * lax.rem(k, 2)) * lax.div(k + 1, 2)


def low_half(shape):
    return lax.broadcasted_iota(jnp.int32, shape, 1) < 64


def pair_up(first, second):
    low = low_half(first.shape)
    return (
        jnp.where(low, first, pltpu.roll(second, 64, 1)),
        jnp.where(low, pltpu.roll(first, 64, 1), second),
    )


def column(row_ref):
    n = row_ref.shape[1]
    return jnp.transpose(jnp.broadcast_to(row_ref[...], (128, n)))


def kernel(
    pair,
    gain1,
    bias1,
    base,
    down,
    up,
    mag,
    wg,
    wo,
    gain2,
    bias2,
    cot,
    update,
    pig,
    gdown,
    gup,
    gmag,
    s1,
    r1,
    s2,
    r2,
    s3,
    r3,
    s4,
    r4,
    amat,
    bmat,
    dbsend,
    dbrecv,
    big,
    mid,
    half,
    dbs,
    sa,
    va,
    sb,
    vb,
    zhat1,
    inv1,
    zbt,
    gate,
    cott,
    dgp,
    dproj,
    vmat,
    wmat,
    wmat_t,
    gain1c,
    gain2c,
    bias2c,
    parts,
    level1,
    level2,
    whole,
    ssem,
    rsem,
    sibsem,
    redsem,
):
    row = lax.axis_index("row")
    q = lax.axis_index("col")
    m = lax.div(row, 2)
    h = lax.rem(row, 2)
    z = lax.div(m, 2)
    x = lax.div(q, 2)
    y = lax.rem(q, 2) * 2 + lax.rem(m, 2)
    me = m * 8 + q
    sibling = (m * 2 + 1 - h, q)

    def chip_at(dz, dy, dx):
        z2 = lax.rem(z + dz, NZ)
        y2 = lax.rem(y + dy, NY)
        x2 = lax.rem(x + dx, NX)
        return z2 * 2 + lax.rem(y2, 2), x2 * 2 + lax.div(y2, 2)

    def chip_by(t):
        return chip_at(
            far_first(lax.div(t, 16), NZ),
            far_first(lax.rem(lax.div(t, 4), 4), NY),
            far_first(lax.rem(t, 4), NX),
        )

    barrier = pltpu.get_barrier_semaphore()

    def greet(t, carry):
        m2, q2 = chip_by(t)
        pl.semaphore_signal(barrier, inc=1, device_id=(m2 * 2 + h, q2), device_id_type=MESH)
        return carry

    lax.fori_loop(0, 127, greet, 0)

    def greet_other(t, carry):
        m2, q2 = chip_at(t, 0, 0)
        pl.semaphore_signal(barrier, inc=1, device_id=(m2 * 2 + 1 - h, q2), device_id_type=MESH)
        return carry

    lax.fori_loop(0, NZ, greet_other, 0)

    v = base[...] + dot(down[...], up[...], precision=HIGHEST)
    nrm = jnp.sqrt(jnp.sum(v * v, axis=0, keepdims=True) + 1e-06)
    scale = mag[...] / nrm
    vmat[...] = v
    w = (v * scale).astype(BF16)
    wmat[...] = w
    wmat_t[...] = jnp.transpose(w.astype(F32)).astype(BF16)
    wg_t = jnp.transpose(wg[...].astype(F32)).astype(BF16)
    gain1c[...] = column(gain1)
    bias1c = column(bias1)
    gain2c[...] = column(gain2)
    bias2c[...] = column(bias2)

    for s in range(8):
        lanes = pl.ds(s * 128, 128)
        zs = jnp.concatenate([pair[s], pair[8 + s]], axis=0).astype(F32)
        zs = jnp.transpose(zs)
        mean = jnp.mean(zs, axis=0, keepdims=True)
        centred = zs - mean
        inv = lax.rsqrt(jnp.mean(centred * centred, axis=0, keepdims=True) + 1e-05)
        zh = centred * inv
        zhat1[:, lanes] = zh
        inv1[:, lanes] = inv
        zb = (zh * gain1c[...] + bias1c).astype(BF16)
        zbt[:, lanes] = zb
        proj = dot(wmat_t[...], zb)
        sig_a = jax.nn.sigmoid(proj[0:128])
        sig_b = jax.nn.sigmoid(proj[256:384])
        sa[:, lanes] = sig_a
        va[:, lanes] = proj[128:256]
        sb[:, lanes] = sig_b
        vb[:, lanes] = proj[384:512]
        big[pl.ds(s, CH, stride=16), :] = sig_a * proj[128:256]
        big[pl.ds(8 + s, CH, stride=16), :] = sig_b * proj[384:512]
    s1[...] = big[...].reshape(CH, 16, 128).astype(BF16)

    pl.semaphore_wait(barrier, 127 + NZ)

    def exchange(step, src, dst_slot):
        local = pltpu.make_async_copy(src(m, q), dst_slot, rsem.at[step])
        local.start()

        def send(t, carry):
            m2, q2 = chip_by(t)
            pltpu.make_async_remote_copy(
                src_ref=src(m2, q2),
                dst_ref=dst_slot,
                send_sem=ssem.at[step],
                recv_sem=rsem.at[step],
                device_id=(m2 * 2 + h, q2),
                device_id_type=MESH,
            ).start()
            return carry

        lax.fori_loop(0, 127, send, 0)

    def arrived(step, ref):
        pltpu.make_async_copy(ref, ref, rsem.at[step]).wait()

    def sent(step, ref):
        pltpu.make_async_copy(ref, ref, ssem.at[step]).wait()

    exchange(0, lambda m2, q2: s1.at[m2 * 8 + q2], r1.at[q, m])

    for s in range(8):
        lanes = pl.ds(s * 128, 128)
        gate[:, lanes] = jax.nn.sigmoid(dot(wg_t, zbt[:, lanes]))
        cs = jnp.concatenate([cot[s], cot[8 + s]], axis=0).astype(F32)
        cott[:, lanes] = jnp.transpose(cs)

    arrived(0, r1)

    for p in range(4):
        lanes = pl.ds(p * 128, 128)
        first = r1[2 * p].astype(F32)
        second = r1[2 * p + 1].astype(F32)
        for part in range(2):
            rows = slice(part * 8, part * 8 + 8)
            even, odd = pair_up(
                first[:, rows, :].reshape(128, 128), second[:, rows, :].reshape(128, 128)
            )
            target = half if part == 0 else mid
            target[:, 0:8, lanes] = even.reshape(16, 8, 128)
            target[:, 8:16, lanes] = odd.reshape(16, 8, 128)
    bmat[:, pl.ds(h, 1)] = mid[...].astype(BF16).reshape(16, 1, 16, TOKENS)
    bcopy = pltpu.make_async_remote_copy(
        src_ref=bmat.at[:, h],
        dst_ref=bmat.at[:, h],
        send_sem=sibsem.at[0],
        recv_sem=sibsem.at[1],
        device_id=sibling,
        device_id_type=MESH,
    )
    bcopy.start()
    amat[...] = half[...].reshape(256, TOKENS).astype(BF16)
    bcopy.wait()

    def split(value, p):
        first, second = pair_up(
            value[:, 0:8, :].reshape(128, 128), value[:, 8:16, :].reshape(128, 128)
        )
        return first.reshape(16, 8, 128), second.reshape(16, 8, 128)

    ball = bmat[...].reshape(TOKENS, TOKENS)
    xs = dot(amat[...], ball, 1, 1)
    for p in range(4):
        block = xs[:, p * 128 : (p + 1) * 128].reshape(16, 16, 128)
        first, second = split(block, p)
        s2[2 * p] = first.astype(BF16)
        s2[2 * p + 1] = second.astype(BF16)
    exchange(1, lambda m2, q2: s2.at[q2, m2], r2.at[me])
    arrived(1, r2)

    big[0:1024] = r2[...].astype(F32).reshape(1024, 128)
    wo_t = jnp.transpose(wo[...].astype(F32)).astype(BF16)
    for s in range(8):
        lanes = pl.ds(s * 128, 128)
        xsl = big[pl.ds(s, CH, stride=8), :]
        mean = jnp.mean(xsl, axis=0, keepdims=True)
        centred = xsl - mean
        inv = lax.rsqrt(jnp.mean(centred * centred, axis=0, keepdims=True) + 1e-05)
        xhat = centred * inv
        xb = (xhat * gain2c[...] + bias2c[...]).astype(BF16)
        outp = dot(wo_t, xb)
        g = gate[:, lanes]
        c = cott[:, lanes]
        up_cells = jnp.transpose(g * outp).astype(BF16)
        update[s] = up_cells[0:64]
        update[8 + s] = up_cells[64:128]
        e = (c * g).astype(BF16)
        dgp[:, lanes] = (c * outp * g * (1.0 - g)).astype(BF16)
        dxh = dot(wo[...], e) * gain2c[...]
        dx = inv * (
            dxh
            - jnp.mean(dxh, axis=0, keepdims=True)
            - xhat * jnp.mean(dxh * xhat, axis=0, keepdims=True)
        )
        big[pl.ds(1024 + s, CH, stride=8), :] = dx
    s3[...] = big[1024:2048].reshape(CH, 8, 128).astype(BF16)
    exchange(2, lambda m2, q2: s3.at[m2 * 8 + q2], r3.at[q, m])
    arrived(2, r3)

    for p in range(4):
        lanes = pl.ds(p * 128, 128)
        even, odd = pair_up(
            r3[2 * p].astype(F32).reshape(128, 128), r3[2 * p + 1].astype(F32).reshape(128, 128)
        )
        half[:, 0:8, lanes] = even.reshape(16, 8, 128)
        half[:, 8:16, lanes] = odd.reshape(16, 8, 128)
    dxm = half[...].reshape(256, TOKENS)
    dxm_t = jnp.transpose(dxm).astype(BF16)
    dbs[...] = dot(dxm_t, amat[...]).reshape(16, 2, 16, TOKENS)
    dbsend[...] = dbs[:, pl.ds(1 - h, 1)].reshape(16, 16, TOKENS).astype(BF16)
    dcopy = pltpu.make_async_remote_copy(
        src_ref=dbsend,
        dst_ref=dbrecv,
        send_sem=sibsem.at[2],
        recv_sem=sibsem.at[3],
        device_id=sibling,
        device_id_type=MESH,
    )
    dcopy.start()
    half[...] = dot(dxm.astype(BF16), bmat[...].reshape(TOKENS, TOKENS)).reshape(16, 16, TOKENS)
    dcopy.wait()
    mid[...] = dbs[:, pl.ds(h, 1)].reshape(16, 16, TOKENS) + dbrecv[...].astype(F32)
    for p in range(4):
        lanes = pl.ds(p * 128, 128)
        a0, a1 = split(half[:, :, lanes], p)
        b0, b1 = split(mid[:, :, lanes], p)
        s4[2 * p] = jnp.concatenate([a0, b0], axis=1).astype(BF16)
        s4[2 * p + 1] = jnp.concatenate([a1, b1], axis=1).astype(BF16)
    exchange(3, lambda m2, q2: s4.at[q2, m2], r4.at[me])
    arrived(3, r4)

    big[...] = r4[...].astype(F32).reshape(2048, 128)
    for s in range(8):
        lanes = pl.ds(s * 128, 128)
        das = big[pl.ds(s, CH, stride=16), :]
        dbl = big[pl.ds(8 + s, CH, stride=16), :]
        sig_a = sa[:, lanes]
        sig_b = sb[:, lanes]
        dproj[0:128, lanes] = (das * va[:, lanes] * sig_a * (1.0 - sig_a)).astype(BF16)
        dproj[128:256, lanes] = (das * sig_a).astype(BF16)
        dproj[256:384, lanes] = (dbl * vb[:, lanes] * sig_b * (1.0 - sig_b)).astype(BF16)
        dproj[384:512, lanes] = (dbl * sig_b).astype(BF16)

    dw = dot(zbt[...], dproj[...], 1, 1) * (1.0 / TOKENS)
    v = vmat[...]
    nrm = jnp.sqrt(jnp.sum(v * v, axis=0, keepdims=True) + 1e-06)
    scale = mag[...] / nrm
    p_sum = jnp.sum(dw * v, axis=0, keepdims=True)
    dv = dw * scale - v * (mag[...] * p_sum / (nrm * nrm * nrm))
    down_t = jnp.transpose(down[...])
    gd = dot(up[...], dv, 1, 1, precision=HIGHEST)
    gu = dot(down_t, dv, precision=HIGHEST)
    gm = p_sum / nrm
    parts[0] = gd[0:8]
    parts[1] = gd[8:16]
    for p in range(4):
        parts[2 + 2 * p] = gu[0:8, p * 128 : (p + 1) * 128]
        parts[3 + 2 * p] = gu[8:16, p * 128 : (p + 1) * 128]
        parts[10, p : p + 1] = gm[:, p * 128 : (p + 1) * 128]
    parts[10, 4:8] = jnp.zeros((4, 128), F32)
    parts[11:16] = jnp.zeros((5, 8, 128), F32)

    g_me = z * 2 + h
    f_me = y * 4 + x

    def in_column(g):
        z2 = lax.div(g, 2)
        return (z2 * 2 + lax.rem(m, 2)) * 2 + lax.rem(g, 2), q

    def in_plane(f):
        y2 = lax.div(f, 4)
        x2 = lax.rem(f, 4)
        return (z * 2 + lax.rem(y2, 2)) * 2 + h, x2 * 2 + lax.div(y2, 2)

    def spread(step, own, src, dst, where):
        local = pltpu.make_async_copy(src(own), dst, redsem.at[step, 1])
        local.start()

        def send(t, carry):
            other = lax.rem(own + t, 16)
            pltpu.make_async_remote_copy(
                src_ref=src(other),
                dst_ref=dst,
                send_sem=redsem.at[step, 0],
                recv_sem=redsem.at[step, 1],
                device_id=where(other),
                device_id_type=MESH,
            ).start()
            return carry

        lax.fori_loop(1, 16, send, 0)

    def gathered(step, ref):
        pltpu.make_async_copy(ref, ref, redsem.at[step, 1]).wait()

    spread(0, g_me, lambda g: parts.at[g], level1.at[g_me], in_column)

    def pair_gradient(s):
        lanes = pl.ds(s * 128, 128)
        dzb = dot(wmat[...], dproj[:, lanes]) + dot(wg[...], dgp[:, lanes])
        dzh = dzb * gain1c[...]
        zh = zhat1[:, lanes]
        dz = inv1[:, lanes] * (
            dzh
            - jnp.mean(dzh, axis=0, keepdims=True)
            - zh * jnp.mean(dzh * zh, axis=0, keepdims=True)
        )
        cells = jnp.transpose(dz).astype(BF16)
        pig[s] = cells[0:64]
        pig[8 + s] = cells[64:128]

    for s in range(0, 4):
        pair_gradient(s)
    gathered(0, level1)
    level1[0] = jnp.sum(level1[...], axis=0)
    spread(1, f_me, lambda f: level1.at[0], level2.at[f_me], in_plane)
    for s in range(4, 8):
        pair_gradient(s)
    gathered(1, level2)
    level2[0] = jnp.sum(level2[...], axis=0)
    spread(2, g_me, lambda g: level2.at[0], whole.at[g_me], in_column)
    gathered(2, whole)

    gdown[...] = jnp.transpose(whole[0:2].reshape(16, 128))
    for p in range(4):
        gup[:, p * 128 : (p + 1) * 128] = whole[2 + 2 * p : 4 + 2 * p].reshape(16, 128)
        gmag[:, p * 128 : (p + 1) * 128] = whole[10, p : p + 1]

    sent(0, s1.at[0:127])
    sent(1, r2.at[0:127])
    sent(2, s3.at[0:127])
    sent(3, r4.at[0:127])
    for step in range(3):
        pltpu.make_async_copy(
            parts.at[0:15], parts.at[0:15], redsem.at[step, 0]
        ).wait()


def on_device(
    pair,
    input_norm_gain,
    input_norm_bias,
    frozen_base_weight,
    adapter_down_factor,
    adapter_up_factor,
    magnitude,
    output_gate_weight,
    output_projection_weight,
    centre_norm_gain,
    centre_norm_bias,
    cotangent,
):
    vmem = pl.BlockSpec(memory_space=pltpu.VMEM)
    cells = (CH, 1024)
    update, pig, gdown, gup, gmag = pl.pallas_call(
        kernel,
        out_shape=(
            jax.ShapeDtypeStruct(pair.shape, BF16),
            jax.ShapeDtypeStruct(pair.shape, BF16),
            jax.ShapeDtypeStruct((CH, 16), F32),
            jax.ShapeDtypeStruct((16, 4 * CH), F32),
            jax.ShapeDtypeStruct((1, 4 * CH), F32),
        ),
        in_specs=[vmem] * 12,
        out_specs=(vmem,) * 5,
        scratch_shapes=[
            pltpu.VMEM((CH, 16, 128), BF16),
            pltpu.VMEM((8, 16, 16, 128), BF16),
            pltpu.VMEM((8, 16, 8, 128), BF16),
            pltpu.VMEM((CH, 8, 128), BF16),
            pltpu.VMEM((CH, 8, 128), BF16),
            pltpu.VMEM((8, 16, 8, 128), BF16),
            pltpu.VMEM((8, 16, 16, 128), BF16),
            pltpu.VMEM((CH, 16, 128), BF16),
            pltpu.VMEM((256, TOKENS), BF16),
            pltpu.VMEM((16, 2, 16, TOKENS), BF16),
            pltpu.VMEM((16, 16, TOKENS), BF16),
            pltpu.VMEM((16, 16, TOKENS), BF16),
            pltpu.VMEM((2048, 128), F32),
            pltpu.VMEM((16, 16, TOKENS), F32),
            pltpu.VMEM((16, 16, TOKENS), F32),
            pltpu.VMEM((16, 2, 16, TOKENS), F32),
            pltpu.VMEM(cells, F32),
            pltpu.VMEM(cells, F32),
            pltpu.VMEM(cells, F32),
            pltpu.VMEM(cells, F32),
            pltpu.VMEM(cells, F32),
            pltpu.VMEM((1, 1024), F32),
            pltpu.VMEM(cells, BF16),
            pltpu.VMEM(cells, F32),
            pltpu.VMEM(cells, F32),
            pltpu.VMEM(cells, BF16),
            pltpu.VMEM((4 * CH, 1024), BF16),
            pltpu.VMEM((CH, 4 * CH), F32),
            pltpu.VMEM((CH, 4 * CH), BF16),
            pltpu.VMEM((4 * CH, CH), BF16),
            pltpu.VMEM((CH, 128), F32),
            pltpu.VMEM((CH, 128), F32),
            pltpu.VMEM((CH, 128), F32),
            pltpu.VMEM((16, 8, 128), F32),
            pltpu.VMEM((16, 8, 128), F32),
            pltpu.VMEM((16, 8, 128), F32),
            pltpu.VMEM((16, 8, 128), F32),
            pltpu.SemaphoreType.DMA((4,)),
            pltpu.SemaphoreType.DMA((4,)),
            pltpu.SemaphoreType.DMA((4,)),
            pltpu.SemaphoreType.DMA((3, 2)),
        ],
        compiler_params=pltpu.CompilerParams(
            collective_id=0, has_side_effects=True, vmem_limit_bytes=48 * 2**20
        ),
    )(
        pair,
        input_norm_gain.reshape(1, CH),
        input_norm_bias.reshape(1, CH),
        frozen_base_weight,
        adapter_down_factor,
        adapter_up_factor,
        magnitude.reshape(1, 4 * CH),
        output_gate_weight,
        output_projection_weight,
        centre_norm_gain.reshape(1, CH),
        centre_norm_bias.reshape(1, CH),
        cotangent,
    )
    return update, pig, gdown, gup, gmag.reshape(4 * CH)


def solution(mesh):
    cells = P("row", "col", None)
    placed = (cells,) + (P(),) * 10 + (cells,)
    return jax.shard_map(
        on_device,
        mesh=mesh,
        in_specs=placed,
        out_specs=(cells, cells, P(), P(), P()),
        check_vma=False,
    )
```

```python
import jax
import jax.numpy as jnp
from jax import lax
from jax.experimental import pallas as pl
from jax.experimental.pallas import tpu as pltpu
from jax.sharding import PartitionSpec as P

MESH = pl.DeviceIdType.MESH
F32 = jnp.float32
BF16 = jnp.bfloat16
NZ, NY, NX = 8, 4, 4
CH = 128
TOKENS = 512
VMEM_GRANT = 63 * 2**20
HIGHEST = lax.Precision.HIGHEST
FAR_Z = (4, 3, 5, 2, 6, 1, 7, 0)
FAR_PLANE = sorted(
    ((dy, dx) for dy in range(NY) for dx in range(NX)),
    key=lambda o: -(min(o[0], NY - o[0]) + min(o[1], NX - o[1])),
)
FAR_COLUMN = sorted(
    ((dz, dh) for dz in range(NZ) for dh in range(2)),
    key=lambda o: -(2 * min(o[0], NZ - o[0]) + o[1]),
)


def dot(a, b, ca=1, cb=0, precision=None):
    return lax.dot_general(
        a, b, (((ca,), (cb,)), ((), ())), precision=precision, preferred_element_type=F32
    )


def far_first(k, n):
    return n // 2 + (1 - 2 * lax.rem(k, 2)) * lax.div(k + 1, 2)


def low_half(shape):
    return lax.broadcasted_iota(jnp.int32, shape, 1) < 64


def pair_up(first, second):
    low = low_half(first.shape)
    return (
        jnp.where(low, first, pltpu.roll(second, 64, 1)),
        jnp.where(low, pltpu.roll(first, 64, 1), second),
    )


def column(row_ref):
    n = row_ref.shape[1]
    return jnp.transpose(jnp.broadcast_to(row_ref[...], (128, n)))


def kernel(*refs):
    operands, (update_out, pig_out, whole), scratch = refs[:12], refs[12:15], refs[15:]
    (
        pair,
        gain1,
        bias1,
        base,
        down_t,
        up,
        mag,
        wg,
        wo,
        gain2,
        bias2,
        cot,
        update,
        pig,
        s1a,
        s1b,
        r1a,
        r1b,
        s2,
        r2,
        s3,
        r3,
        s4a,
        s4b,
        r4a,
        r4b,
        amat,
        bmat,
        dbsend,
        dbrecv,
        big_a,
        big_b,
        mid,
        half,
        dbs,
        sa,
        va,
        sb,
        vb,
        zhat1,
        inv1,
        zbt,
        gate,
        cott,
        dgp,
        dproj,
        vmat,
        wmat,
        wmat_t,
        gain1c,
        gain2c,
        bias2c,
        parts,
        level1,
        level2,
        ssem,
        rsem,
        sibsem,
        redsem,
        insem,
        outsem,
    ) = scratch
    local = (pair, gain1, bias1, base, down_t, up, mag, wg, wo, gain2, bias2, cot)
    row = lax.axis_index("row")
    q = lax.axis_index("col")
    m = lax.div(row, 2)
    h = lax.rem(row, 2)
    z = lax.div(m, 2)
    x = lax.div(q, 2)
    y = lax.rem(q, 2) * 2 + lax.rem(m, 2)
    me = m * 8 + q
    sibling = (m * 2 + 1 - h, q)

    def chip_at(dz, dy, dx):
        z2 = lax.rem(z + dz, NZ)
        y2 = lax.rem(y + dy, NY)
        x2 = lax.rem(x + dx, NX)
        return z2 * 2 + lax.rem(y2, 2), x2 * 2 + lax.div(y2, 2)

    z_rows = [4 * lax.rem(z + dz, NZ) + h for dz in FAR_Z]

    def plane(t):
        y2 = lax.rem(y + far_first(lax.div(t, 4), NY), NY)
        x2 = lax.rem(x + far_first(lax.rem(t, 4), NX), NX)
        return 2 * lax.rem(y2, 2), x2 * 2 + lax.div(y2, 2)

    def to_all(act):
        def over_plane(t, carry):
            parity, q2 = plane(t)
            for z_row in z_rows:
                act(z_row + parity, q2)
            return carry

        lax.fori_loop(0, 15, over_plane, 0)
        parity, q2 = plane(15)
        for z_row in z_rows[:-1]:
            act(z_row + parity, q2)

    barrier = pltpu.get_barrier_semaphore()

    def greet(row2, q2):
        pl.semaphore_signal(barrier, inc=1, device_id=(row2, q2), device_id_type=MESH)

    to_all(greet)
    for z_row in z_rows:
        greet(z_row + 2 * lax.rem(y, 2) + 1 - 2 * h, q)

    loads = [
        pltpu.make_async_copy(operand, here, insem.at[n])
        for n, (operand, here) in enumerate(zip(operands, local))
    ]
    for load in loads:
        load.start()
    for load in loads:
        load.wait()
    pending = []

    def finish():
        for wait in pending:
            wait()

    v = base[...] + dot(down_t[...], up[...], 0, 0, precision=HIGHEST)
    nrm = jnp.sqrt(jnp.sum(v * v, axis=0, keepdims=True) + 1e-06)
    scale = mag[...] / nrm
    vmat[...] = v
    w = (v * scale).astype(BF16)
    wmat[...] = w
    wmat_t[...] = jnp.transpose(w.astype(F32)).astype(BF16)
    wg_t = jnp.transpose(wg[...].astype(F32)).astype(BF16)
    gain1c[...] = column(gain1)
    bias1c = column(bias1)
    gain2c[...] = column(gain2)
    bias2c[...] = column(bias2)

    for s in range(8):
        lanes = pl.ds(s * 128, 128)
        zs = jnp.concatenate([pair[s], pair[8 + s]], axis=0).astype(F32)
        zs = jnp.transpose(zs)
        mean = jnp.mean(zs, axis=0, keepdims=True)
        centred = zs - mean
        inv = lax.rsqrt(jnp.mean(centred * centred, axis=0, keepdims=True) + 1e-05)
        zh = centred * inv
        zhat1[:, lanes] = zh
        inv1[:, lanes] = inv
        zb = (zh * gain1c[...] + bias1c).astype(BF16)
        zbt[:, lanes] = zb
        proj = dot(wmat_t[...], zb)
        sig_a = jax.nn.sigmoid(proj[0:128])
        sig_b = jax.nn.sigmoid(proj[256:384])
        sa[:, lanes] = sig_a
        va[:, lanes] = proj[128:256]
        sb[:, lanes] = sig_b
        vb[:, lanes] = proj[384:512]
        big_a[pl.ds(s, CH, stride=8), :] = sig_a * proj[128:256]
        big_b[pl.ds(s, CH, stride=8), :] = sig_b * proj[384:512]
    s1b[...] = big_b[...].reshape(CH, 8, 128).astype(BF16)
    s1a[...] = big_a[...].reshape(CH, 8, 128).astype(BF16)

    pl.semaphore_wait(barrier, 127 + NZ)

    def exchange(step, src, dst_slot, received):
        own = pltpu.make_async_copy(src(m, q), dst_slot, rsem.at[step])
        own.start()

        def send(row2, q2):
            pltpu.make_async_remote_copy(
                src_ref=src(lax.div(row2, 2), q2),
                dst_ref=dst_slot,
                send_sem=ssem.at[step],
                recv_sem=rsem.at[step],
                device_id=(row2, q2),
                device_id_type=MESH,
            ).start()

        to_all(send)
        others = s1a.at[0:127]
        pending.append(pltpu.make_async_copy(others, others, ssem.at[step]).wait)
        return pltpu.make_async_copy(received, received, rsem.at[step]).wait

    b_here = exchange(0, lambda m2, q2: s1b.at[m2 * 8 + q2], r1b.at[q, m], r1b)
    a_here = exchange(1, lambda m2, q2: s1a.at[m2 * 8 + q2], r1a.at[q, m], r1a)

    for s in range(8):
        lanes = pl.ds(s * 128, 128)
        gate[:, lanes] = jax.nn.sigmoid(dot(wg_t, zbt[:, lanes]))
        cs = jnp.concatenate([cot[s], cot[8 + s]], axis=0).astype(F32)
        cott[:, lanes] = jnp.transpose(cs)

    def assemble(received, target):
        for p in range(4):
            lanes = pl.ds(p * 128, 128)
            even, odd = pair_up(
                received[2 * p].astype(F32).reshape(128, 128),
                received[2 * p + 1].astype(F32).reshape(128, 128),
            )
            target[:, 0:8, lanes] = even.reshape(16, 8, 128)
            target[:, 8:16, lanes] = odd.reshape(16, 8, 128)

    def to_sibling(n, src, dst):
        copy = pltpu.make_async_remote_copy(
            src_ref=src,
            dst_ref=dst,
            send_sem=sibsem.at[2 * n],
            recv_sem=sibsem.at[2 * n + 1],
            device_id=sibling,
            device_id_type=MESH,
        )
        copy.start()
        return copy.wait

    b_here()
    assemble(r1b, mid)
    bmat[:, pl.ds(h, 1)] = mid[...].astype(BF16).reshape(16, 1, 16, TOKENS)
    b_whole = to_sibling(0, bmat.at[:, h], bmat.at[:, h])
    a_here()
    assemble(r1a, half)
    amat[...] = half[...].reshape(256, TOKENS).astype(BF16)
    b_whole()

    def split(value, p):
        first, second = pair_up(
            value[:, 0:8, :].reshape(128, 128), value[:, 8:16, :].reshape(128, 128)
        )
        return first.reshape(16, 8, 128), second.reshape(16, 8, 128)

    ball = bmat[...].reshape(TOKENS, TOKENS)
    xs = dot(amat[...], ball, 1, 1)
    for p in range(4):
        block = xs[:, p * 128 : (p + 1) * 128].reshape(16, 16, 128)
        first, second = split(block, p)
        s2[2 * p] = first.astype(BF16)
        s2[2 * p + 1] = second.astype(BF16)
    x_here = exchange(2, lambda m2, q2: s2.at[q2, m2], r2.at[me], r2)
    x_here()

    big_a[...] = r2[...].astype(F32).reshape(1024, 128)
    wo_t = jnp.transpose(wo[...].astype(F32)).astype(BF16)
    for s in range(8):
        lanes = pl.ds(s * 128, 128)
        xsl = big_a[pl.ds(s, CH, stride=8), :]
        mean = jnp.mean(xsl, axis=0, keepdims=True)
        centred = xsl - mean
        inv = lax.rsqrt(jnp.mean(centred * centred, axis=0, keepdims=True) + 1e-05)
        xhat = centred * inv
        xb = (xhat * gain2c[...] + bias2c[...]).astype(BF16)
        outp = dot(wo_t, xb)
        g = gate[:, lanes]
        c = cott[:, lanes]
        up_cells = jnp.transpose(g * outp).astype(BF16)
        update[s] = up_cells[0:64]
        update[8 + s] = up_cells[64:128]
        e = (c * g).astype(BF16)
        dgp[:, lanes] = (c * outp * g * (1.0 - g)).astype(BF16)
        dxh = dot(wo[...], e) * gain2c[...]
        dx = inv * (
            dxh
            - jnp.mean(dxh, axis=0, keepdims=True)
            - xhat * jnp.mean(dxh * xhat, axis=0, keepdims=True)
        )
        big_b[pl.ds(s, CH, stride=8), :] = dx
    s3[...] = big_b[...].reshape(CH, 8, 128).astype(BF16)
    dx_here = exchange(3, lambda m2, q2: s3.at[m2 * 8 + q2], r3.at[q, m], r3)
    update_away = pltpu.make_async_copy(update, update_out, outsem.at[0])
    update_away.start()
    pending.append(update_away.wait)
    dx_here()

    assemble(r3, half)
    dxm = half[...].reshape(256, TOKENS)
    da = dot(dxm.astype(BF16), bmat[...].reshape(TOKENS, TOKENS)).reshape(16, 16, TOKENS)
    for p in range(4):
        first, second = split(da[:, :, p * 128 : (p + 1) * 128], p)
        s4a[2 * p] = first.astype(BF16)
        s4a[2 * p + 1] = second.astype(BF16)
    da_here = exchange(4, lambda m2, q2: s4a.at[q2, m2], r4a.at[me], r4a)
    dxm_t = jnp.transpose(dxm).astype(BF16)
    dbs[...] = dot(dxm_t, amat[...]).reshape(16, 2, 16, TOKENS)
    dbsend[...] = dbs[:, pl.ds(1 - h, 1)].reshape(16, 16, TOKENS).astype(BF16)
    db_whole = to_sibling(1, dbsend, dbrecv)
    db_whole()
    mid[...] = dbs[:, pl.ds(h, 1)].reshape(16, 16, TOKENS) + dbrecv[...].astype(F32)
    for p in range(4):
        first, second = split(mid[:, :, pl.ds(p * 128, 128)], p)
        s4b[2 * p] = first.astype(BF16)
        s4b[2 * p + 1] = second.astype(BF16)
    db_here = exchange(5, lambda m2, q2: s4b.at[q2, m2], r4b.at[me], r4b)

    def through_gate(received, big, sig_ref, val_ref, first):
        big[...] = received[...].astype(F32).reshape(1024, 128)
        for s in range(8):
            lanes = pl.ds(s * 128, 128)
            d = big[pl.ds(s, CH, stride=8), :]
            sig = sig_ref[:, lanes]
            dproj[first : first + 128, lanes] = (
                d * val_ref[:, lanes] * sig * (1.0 - sig)
            ).astype(BF16)
            dproj[first + 128 : first + 256, lanes] = (d * sig).astype(BF16)

    da_here()
    through_gate(r4a, big_a, sa, va, 0)
    db_here()
    through_gate(r4b, big_b, sb, vb, 256)

    dw = dot(zbt[...], dproj[...], 1, 1) * (1.0 / TOKENS)
    v = vmat[...]
    nrm = jnp.sqrt(jnp.sum(v * v, axis=0, keepdims=True) + 1e-06)
    scale = mag[...] / nrm
    p_sum = jnp.sum(dw * v, axis=0, keepdims=True)
    dv = dw * scale - v * (mag[...] * p_sum / (nrm * nrm * nrm))
    gd = dot(up[...], dv, 1, 1, precision=HIGHEST)
    gu = dot(down_t[...], dv, precision=HIGHEST)
    gm = p_sum / nrm
    parts[0] = gd[0:8]
    parts[1] = gd[8:16]
    for p in range(4):
        parts[2 + 2 * p] = gu[0:8, p * 128 : (p + 1) * 128]
        parts[3 + 2 * p] = gu[8:16, p * 128 : (p + 1) * 128]
        parts[10, p : p + 1] = gm[:, p * 128 : (p + 1) * 128]
    parts[10, 4:8] = jnp.zeros((4, 128), F32)
    parts[11:16] = jnp.zeros((5, 8, 128), F32)

    f_me = y * 4 + x
    g_me = z * 2 + h

    def in_plane(offset):
        y2 = lax.rem(y + offset[0], NY)
        x2 = lax.rem(x + offset[1], NX)
        device = (4 * z + 2 * lax.rem(y2, 2) + h, x2 * 2 + lax.div(y2, 2))
        return device, y2 * 4 + x2

    def in_column(offset):
        z2 = lax.rem(z + offset[0], NZ)
        h2 = 1 - h if offset[1] else h
        return (4 * z2 + 2 * lax.rem(y, 2) + h2, q), z2 * 2 + h2

    def spread(step, offsets, where, src, own, dst, received):
        pltpu.make_async_copy(src(own), dst, redsem.at[step, 1]).start()
        for offset in offsets:
            if offset == (0, 0):
                continue
            device, other = where(offset)
            pltpu.make_async_remote_copy(
                src_ref=src(other),
                dst_ref=dst,
                send_sem=redsem.at[step, 0],
                recv_sem=redsem.at[step, 1],
                device_id=device,
                device_id_type=MESH,
            ).start()
        others = parts.at[0:15]
        pending.append(pltpu.make_async_copy(others, others, redsem.at[step, 0]).wait)
        return pltpu.make_async_copy(received, received, redsem.at[step, 1]).wait

    plane_here = spread(
        0, FAR_PLANE, in_plane, lambda f: parts.at[f], f_me, level1.at[f_me], level1
    )

    def pair_gradient(s):
        lanes = pl.ds(s * 128, 128)
        dzb = dot(wmat[...], dproj[:, lanes]) + dot(wg[...], dgp[:, lanes])
        dzh = dzb * gain1c[...]
        zh = zhat1[:, lanes]
        dz = inv1[:, lanes] * (
            dzh
            - jnp.mean(dzh, axis=0, keepdims=True)
            - zh * jnp.mean(dzh * zh, axis=0, keepdims=True)
        )
        cells = jnp.transpose(dz).astype(BF16)
        pig[s] = cells[0:64]
        pig[8 + s] = cells[64:128]

    for s in range(0, 3):
        pair_gradient(s)
    plane_here()
    level1[0] = jnp.sum(level1[...], axis=0)
    column_here = spread(
        1, FAR_COLUMN, in_column, lambda g: level1.at[0], g_me, level2.at[g_me], level2
    )
    for s in range(3, 8):
        pair_gradient(s)
    pig_away = pltpu.make_async_copy(pig, pig_out, outsem.at[1])
    pig_away.start()
    pending.append(pig_away.wait)
    column_here()
    level2[0] = jnp.sum(level2[...], axis=0)
    whole_here = spread(
        2, FAR_PLANE, in_plane, lambda f: level2.at[0], f_me, whole.at[f_me], whole
    )
    whole_here()
    finish()


def unpack(update_in, pig_in, whole_in, update, pig, gdown, gup, gmag, *scratch):
    here, (insem, outsem) = scratch[:3], scratch[3:]
    loads = [
        pltpu.make_async_copy(src, dst, insem.at[n])
        for n, (src, dst) in enumerate(zip((update_in, pig_in, whole_in), here))
    ]
    for load in loads:
        load.start()
    stores = []
    for n, dst in enumerate((update, pig)):
        loads[n].wait()
        stores.append(pltpu.make_async_copy(here[n], dst, outsem.at[n]))
        stores[n].start()
    loads[2].wait()
    whole = here[2]
    gdown[...] = whole[0:2].reshape(16, 128)
    for p in range(4):
        gup[:, p * 128 : (p + 1) * 128] = whole[2 + 2 * p : 4 + 2 * p].reshape(16, 128)
        gmag[:, p * 128 : (p + 1) * 128] = whole[10, p : p + 1]
    for store in stores:
        store.wait()


def on_device(
    pair,
    input_norm_gain,
    input_norm_bias,
    frozen_base_weight,
    adapter_down_factor,
    adapter_up_factor,
    magnitude,
    output_gate_weight,
    output_projection_weight,
    centre_norm_gain,
    centre_norm_bias,
    cotangent,
):
    vmem = pl.BlockSpec(memory_space=pltpu.VMEM)
    hbm = pl.BlockSpec(memory_space=pltpu.HBM)
    cells = (CH, 1024)
    message = (CH, 8, 128)
    by_chip = (8, 16, 8, 128)
    operands = (
        pair,
        input_norm_gain.reshape(1, CH),
        input_norm_bias.reshape(1, CH),
        frozen_base_weight,
        adapter_down_factor.T,
        adapter_up_factor,
        magnitude.reshape(1, 4 * CH),
        output_gate_weight,
        output_projection_weight,
        centre_norm_gain.reshape(1, CH),
        centre_norm_bias.reshape(1, CH),
        cotangent,
    )
    block = jax.ShapeDtypeStruct(pair.shape, BF16)
    update, pig, whole = pl.pallas_call(
        kernel,
        out_shape=(block, block, jax.ShapeDtypeStruct((16, 8, 128), F32)),
        in_specs=[hbm] * 12,
        out_specs=(hbm, hbm, vmem),
        scratch_shapes=[pltpu.VMEM(a.shape, a.dtype) for a in operands]
        + [
            pltpu.VMEM(pair.shape, BF16),
            pltpu.VMEM(pair.shape, BF16),
            pltpu.VMEM(message, BF16),
            pltpu.VMEM(message, BF16),
            pltpu.VMEM(by_chip, BF16),
            pltpu.VMEM(by_chip, BF16),
            pltpu.VMEM(by_chip, BF16),
            pltpu.VMEM(message, BF16),
            pltpu.VMEM(message, BF16),
            pltpu.VMEM(by_chip, BF16),
            pltpu.VMEM(by_chip, BF16),
            pltpu.VMEM(by_chip, BF16),
            pltpu.VMEM(message, BF16),
            pltpu.VMEM(message, BF16),
            pltpu.VMEM((256, TOKENS), BF16),
            pltpu.VMEM((16, 2, 16, TOKENS), BF16),
            pltpu.VMEM((16, 16, TOKENS), BF16),
            pltpu.VMEM((16, 16, TOKENS), BF16),
            pltpu.VMEM((1024, 128), F32),
            pltpu.VMEM((1024, 128), F32),
            pltpu.VMEM((16, 16, TOKENS), F32),
            pltpu.VMEM((16, 16, TOKENS), F32),
            pltpu.VMEM((16, 2, 16, TOKENS), F32),
            pltpu.VMEM(cells, F32),
            pltpu.VMEM(cells, F32),
            pltpu.VMEM(cells, F32),
            pltpu.VMEM(cells, F32),
            pltpu.VMEM(cells, F32),
            pltpu.VMEM((1, 1024), F32),
            pltpu.VMEM(cells, BF16),
            pltpu.VMEM(cells, F32),
            pltpu.VMEM(cells, F32),
            pltpu.VMEM(cells, BF16),
            pltpu.VMEM((4 * CH, 1024), BF16),
            pltpu.VMEM((CH, 4 * CH), F32),
            pltpu.VMEM((CH, 4 * CH), BF16),
            pltpu.VMEM((4 * CH, CH), BF16),
            pltpu.VMEM((CH, 128), F32),
            pltpu.VMEM((CH, 128), F32),
            pltpu.VMEM((CH, 128), F32),
            pltpu.VMEM((16, 8, 128), F32),
            pltpu.VMEM((16, 8, 128), F32),
            pltpu.VMEM((16, 8, 128), F32),
            pltpu.SemaphoreType.DMA((6,)),
            pltpu.SemaphoreType.DMA((6,)),
            pltpu.SemaphoreType.DMA((4,)),
            pltpu.SemaphoreType.DMA((3, 2)),
            pltpu.SemaphoreType.DMA((12,)),
            pltpu.SemaphoreType.DMA((2,)),
        ],
        compiler_params=pltpu.CompilerParams(
            collective_id=0, has_side_effects=True, vmem_limit_bytes=VMEM_GRANT
        ),
    )(*operands)
    update, pig, gdown, gup, gmag = pl.pallas_call(
        unpack,
        out_shape=(
            block,
            block,
            jax.ShapeDtypeStruct((16, CH), F32),
            jax.ShapeDtypeStruct((16, 4 * CH), F32),
            jax.ShapeDtypeStruct((1, 4 * CH), F32),
        ),
        in_specs=[hbm] * 3,
        out_specs=(hbm, hbm, vmem, vmem, vmem),
        scratch_shapes=[
            pltpu.VMEM(block.shape, BF16),
            pltpu.VMEM(block.shape, BF16),
            pltpu.VMEM((16, 8, 128), F32),
            pltpu.SemaphoreType.DMA((3,)),
            pltpu.SemaphoreType.DMA((2,)),
        ],
        compiler_params=pltpu.CompilerParams(vmem_limit_bytes=VMEM_GRANT),
    )(update, pig, whole)
    return update, pig, gdown.T, gup, gmag.reshape(4 * CH)


def solution(mesh):
    cells = P("row", "col", None)
    placed = (cells,) + (P(),) * 10 + (cells,)
    return jax.shard_map(
        on_device,
        mesh=mesh,
        in_specs=placed,
        out_specs=(cells, cells, P(), P(), P()),
        check_vma=False,
    )
```

```python
import jax
import jax.numpy as jnp
from jax import lax
from jax.experimental import pallas as pl
from jax.experimental.pallas import tpu as pltpu
from jax.sharding import PartitionSpec as P

MESH = pl.DeviceIdType.MESH
F32 = jnp.float32
BF16 = jnp.bfloat16
NZ, NY, NX = 8, 4, 4
CH = 128
TOKENS = 512
VMEM_GRANT = 63 * 2**20
HIGHEST = lax.Precision.HIGHEST
FAR_Z = (4, 3, 5, 2, 6, 1, 7, 0)
FAR_PLANE = sorted(
    ((dy, dx) for dy in range(NY) for dx in range(NX)),
    key=lambda o: -(min(o[0], NY - o[0]) + min(o[1], NX - o[1])),
)
FAR_COLUMN = sorted(
    ((dz, dh) for dz in range(NZ) for dh in range(2)),
    key=lambda o: -(2 * min(o[0], NZ - o[0]) + o[1]),
)


def dot(a, b, ca=1, cb=0, precision=None):
    return lax.dot_general(
        a, b, (((ca,), (cb,)), ((), ())), precision=precision, preferred_element_type=F32
    )


def far_first(k, n):
    return n // 2 + (1 - 2 * lax.rem(k, 2)) * lax.div(k + 1, 2)


def pair_up(first, second):
    last = first.ndim - 1
    low = lax.broadcasted_iota(jnp.int32, first.shape, last) < 64
    return (
        jnp.where(low, first, pltpu.roll(second, 64, last)),
        jnp.where(low, pltpu.roll(first, 64, last), second),
    )


def half_rows(big, u):
    return big[...].reshape(CH, 8, 128)[:, 4 * u : 4 * u + 4, :].astype(BF16)


def column(row_ref):
    n = row_ref.shape[1]
    return jnp.transpose(jnp.broadcast_to(row_ref[...], (128, n)))


def kernel(*refs):
    operands, (update_out, pig_out, whole), scratch = refs[:12], refs[12:15], refs[15:]
    (
        pair,
        gain1,
        bias1,
        base,
        down_t,
        up,
        mag,
        wg,
        wo,
        gain2,
        bias2,
        cot,
        update,
        pig,
        s1a,
        s1b,
        r1a,
        r1b,
        s2,
        r2,
        s3,
        r3,
        s4a,
        s4b,
        r4a,
        r4b,
        amat,
        bmat,
        dbsend,
        dbrecv,
        big_a,
        big_b,
        mid,
        half,
        dbs,
        sa,
        va,
        sb,
        vb,
        zhat1,
        inv1,
        zbt,
        gate,
        cott,
        dgp,
        dproj,
        vmat,
        wmat,
        wmat_t,
        gain1c,
        gain2c,
        bias2c,
        parts,
        level1,
        level2,
        ssem,
        rsem,
        sibsem,
        redsem,
        insem,
        outsem,
    ) = scratch
    local = (pair, gain1, bias1, base, down_t, up, mag, wg, wo, gain2, bias2, cot)
    row = lax.axis_index("row")
    q = lax.axis_index("col")
    m = lax.div(row, 2)
    h = lax.rem(row, 2)
    z = lax.div(m, 2)
    x = lax.div(q, 2)
    y = lax.rem(q, 2) * 2 + lax.rem(m, 2)
    me = m * 8 + q
    sibling = (m * 2 + 1 - h, q)

    def chip_at(dz, dy, dx):
        z2 = lax.rem(z + dz, NZ)
        y2 = lax.rem(y + dy, NY)
        x2 = lax.rem(x + dx, NX)
        return z2 * 2 + lax.rem(y2, 2), x2 * 2 + lax.div(y2, 2)

    z_rows = [4 * lax.rem(z + dz, NZ) + h for dz in FAR_Z]

    def plane(t):
        y2 = lax.rem(y + far_first(lax.div(t, 4), NY), NY)
        x2 = lax.rem(x + far_first(lax.rem(t, 4), NX), NX)
        return 2 * lax.rem(y2, 2), x2 * 2 + lax.div(y2, 2)

    def to_all(act):
        def over_plane(t, carry):
            parity, q2 = plane(t)
            for z_row in z_rows:
                act(z_row + parity, q2)
            return carry

        lax.fori_loop(0, 15, over_plane, 0)
        parity, q2 = plane(15)
        for z_row in z_rows[:-1]:
            act(z_row + parity, q2)

    loads = [
        pltpu.make_async_copy(operand, here, insem.at[n])
        for n, (operand, here) in enumerate(zip(operands, local))
    ]
    for load in loads:
        load.start()

    barrier = pltpu.get_barrier_semaphore()

    def greet(row2, q2):
        pl.semaphore_signal(barrier, inc=1, device_id=(row2, q2), device_id_type=MESH)

    to_all(greet)
    for z_row in z_rows:
        greet(z_row + 2 * lax.rem(y, 2) + 1 - 2 * h, q)

    for load in loads:
        load.wait()
    pending = []

    def finish():
        for wait in pending:
            wait()

    v = base[...] + dot(down_t[...], up[...], 0, 0, precision=HIGHEST)
    nrm = jnp.sqrt(jnp.sum(v * v, axis=0, keepdims=True) + 1e-06)
    scale = mag[...] / nrm
    vmat[...] = v
    w = (v * scale).astype(BF16)
    wmat[...] = w
    wmat_t[...] = jnp.transpose(w.astype(F32)).astype(BF16)
    wg_t = jnp.transpose(wg[...].astype(F32)).astype(BF16)
    gain1c[...] = column(gain1)
    bias1c = column(bias1)
    gain2c[...] = column(gain2)
    bias2c[...] = column(bias2)

    def project(s, zb, first, sig_ref, val_ref, big):
        lanes = pl.ds(s * 128, 128)
        proj = dot(wmat_t[first : first + 256], zb)
        sig = jax.nn.sigmoid(proj[0:128])
        sig_ref[:, lanes] = sig
        val_ref[:, lanes] = proj[128:256]
        big[pl.ds(s, CH, stride=8), :] = sig * proj[128:256]

    for s in range(8):
        lanes = pl.ds(s * 128, 128)
        zs = jnp.concatenate([pair[s], pair[8 + s]], axis=0).astype(F32)
        zs = jnp.transpose(zs)
        mean = jnp.mean(zs, axis=0, keepdims=True)
        centred = zs - mean
        inv = lax.rsqrt(jnp.mean(centred * centred, axis=0, keepdims=True) + 1e-05)
        zh = centred * inv
        zhat1[:, lanes] = zh
        inv1[:, lanes] = inv
        zb = (zh * gain1c[...] + bias1c).astype(BF16)
        zbt[:, lanes] = zb
        project(s, zb, 256, sb, vb, big_b)
    s1b[...] = big_b[...].reshape(CH, 8, 128).astype(BF16)

    pl.semaphore_wait(barrier, 127 + NZ)

    def exchange(step, src, dst_slot, received, others):
        own = pltpu.make_async_copy(src(m, q), dst_slot, rsem.at[step])
        own.start()

        def send(row2, q2):
            pltpu.make_async_remote_copy(
                src_ref=src(lax.div(row2, 2), q2),
                dst_ref=dst_slot,
                send_sem=ssem.at[step],
                recv_sem=rsem.at[step],
                device_id=(row2, q2),
                device_id_type=MESH,
            ).start()

        to_all(send)
        pending.append(pltpu.make_async_copy(others, others, ssem.at[step]).wait)
        return pltpu.make_async_copy(received, received, rsem.at[step]).wait

    def from_cells(step, sent, received):
        return exchange(
            step,
            lambda m2, q2: sent.at[m2 * 8 + q2],
            received.at[q, m],
            received,
            sent.at[0:127],
        )

    def from_owner(step, sent, received):
        return exchange(
            step,
            lambda m2, q2: sent.at[q2, m2],
            received.at[me],
            received,
            received.at[0:127],
        )

    b_here = from_cells(0, s1b, r1b)
    a_here = []
    for u in range(2):
        for s in range(4 * u, 4 * u + 4):
            project(s, zbt[:, pl.ds(s * 128, 128)], 0, sa, va, big_a)
        s1a[u] = half_rows(big_a, u)
        a_here.append(from_cells(1 + u, s1a.at[u], r1a.at[u]))

    for s in range(8):
        lanes = pl.ds(s * 128, 128)
        gate[:, lanes] = jax.nn.sigmoid(dot(wg_t, zbt[:, lanes]))
        cs = jnp.concatenate([cot[s], cot[8 + s]], axis=0).astype(F32)
        cott[:, lanes] = jnp.transpose(cs)

    def assemble(received, target):
        rows = received.shape[2]
        for p in range(4):
            lanes = pl.ds(p * 128, 128)
            even, odd = pair_up(received[2 * p].astype(F32), received[2 * p + 1].astype(F32))
            target[:, 0:rows, lanes] = even
            target[:, rows : 2 * rows, lanes] = odd

    def dispatch(value, messages):
        rows = value.shape[1] // 2
        for p in range(4):
            block = value[:, :, p * 128 : (p + 1) * 128]
            first, second = pair_up(block[:, 0:rows, :], block[:, rows : 2 * rows, :])
            messages[2 * p] = first.astype(BF16)
            messages[2 * p + 1] = second.astype(BF16)

    def to_sibling(n, src, dst):
        copy = pltpu.make_async_remote_copy(
            src_ref=src,
            dst_ref=dst,
            send_sem=sibsem.at[2 * n],
            recv_sem=sibsem.at[2 * n + 1],
            device_id=sibling,
            device_id_type=MESH,
        )
        copy.start()
        return copy.wait

    b_here()
    assemble(r1b, mid)
    bmat[:, pl.ds(h, 1)] = mid[...].astype(BF16).reshape(16, 1, 16, TOKENS)
    b_whole = to_sibling(0, bmat.at[:, h], bmat.at[:, h])
    x_here = []
    for u in range(2):
        a_here[u]()
        assemble(r1a.at[u], half)
        amat[u] = half[...].reshape(128, TOKENS).astype(BF16)
        if u == 0:
            b_whole()
        ball = bmat[...].reshape(TOKENS, TOKENS)
        dispatch(dot(amat[u], ball, 1, 1).reshape(16, 8, TOKENS), s2.at[u])
        x_here.append(from_owner(3 + u, s2.at[u], r2.at[u]))

    wo_t = jnp.transpose(wo[...].astype(F32)).astype(BF16)

    def centre(s):
        lanes = pl.ds(s * 128, 128)
        xsl = big_a[pl.ds(s, CH, stride=8), :]
        mean = jnp.mean(xsl, axis=0, keepdims=True)
        centred = xsl - mean
        inv = lax.rsqrt(jnp.mean(centred * centred, axis=0, keepdims=True) + 1e-05)
        xhat = centred * inv
        xb = (xhat * gain2c[...] + bias2c[...]).astype(BF16)
        outp = dot(wo_t, xb)
        g = gate[:, lanes]
        c = cott[:, lanes]
        up_cells = jnp.transpose(g * outp).astype(BF16)
        update[s] = up_cells[0:64]
        update[8 + s] = up_cells[64:128]
        e = (c * g).astype(BF16)
        dgp[:, lanes] = (c * outp * g * (1.0 - g)).astype(BF16)
        dxh = dot(wo[...], e) * gain2c[...]
        dx = inv * (
            dxh
            - jnp.mean(dxh, axis=0, keepdims=True)
            - xhat * jnp.mean(dxh * xhat, axis=0, keepdims=True)
        )
        big_b[pl.ds(s, CH, stride=8), :] = dx

    def received_half(received, big, u):
        big.reshape(CH, 8, 128)[:, 4 * u : 4 * u + 4, :] = received[...].astype(F32)

    dx_here = []
    for u in range(2):
        x_here[u]()
        received_half(r2.at[u], big_a, u)
        for s in range(4 * u, 4 * u + 4):
            centre(s)
        s3[u] = half_rows(big_b, u)
        dx_here.append(from_cells(5 + u, s3.at[u], r3.at[u]))
    update_away = pltpu.make_async_copy(update, update_out, outsem.at[0])
    update_away.start()
    pending.append(update_away.wait)

    da_here = []
    for u in range(2):
        dx_here[u]()
        assemble(r3.at[u], half)
        dxm = half[...].reshape(128, TOKENS)
        db_part = dot(jnp.transpose(dxm).astype(BF16), amat[u]).reshape(16, 2, 16, TOKENS)
        if u == 0:
            dbs[...] = db_part
        else:
            dbs[...] += db_part
            dbsend[...] = dbs[:, pl.ds(1 - h, 1)].reshape(16, 16, TOKENS).astype(BF16)
            db_whole = to_sibling(1, dbsend, dbrecv)
        da = dot(dxm.astype(BF16), bmat[...].reshape(TOKENS, TOKENS))
        dispatch(da.reshape(16, 8, TOKENS), s4a.at[u])
        da_here.append(from_owner(7 + u, s4a.at[u], r4a.at[u]))
    db_whole()
    mid[...] = dbs[:, pl.ds(h, 1)].reshape(16, 16, TOKENS) + dbrecv[...].astype(F32)
    dispatch(mid[...], s4b)
    db_here = from_owner(9, s4b, r4b)

    def through_gate(s, big, sig_ref, val_ref, first):
        lanes = pl.ds(s * 128, 128)
        d = big[pl.ds(s, CH, stride=8), :]
        sig = sig_ref[:, lanes]
        dproj[first : first + 128, lanes] = (
            d * val_ref[:, lanes] * sig * (1.0 - sig)
        ).astype(BF16)
        dproj[first + 128 : first + 256, lanes] = (d * sig).astype(BF16)

    def weight_part(n):
        half_of = slice(n * 256, n * 256 + 256)
        dw = dot(zbt[...], dproj[half_of, :], 1, 1) * (1.0 / TOKENS)
        v = vmat[:, half_of]
        mg = mag[:, half_of]
        nrm = jnp.sqrt(jnp.sum(v * v, axis=0, keepdims=True) + 1e-06)
        p_sum = jnp.sum(dw * v, axis=0, keepdims=True)
        dv = dw * (mg / nrm) - v * (mg * p_sum / (nrm * nrm * nrm))
        gu = dot(down_t[...], dv, precision=HIGHEST)
        gm = p_sum / nrm
        for p in range(2):
            lanes = slice(p * 128, p * 128 + 128)
            parts[2 + 4 * n + 2 * p] = gu[0:8, lanes]
            parts[3 + 4 * n + 2 * p] = gu[8:16, lanes]
            parts[10, 2 * n + p : 2 * n + p + 1] = gm[:, lanes]
        return dot(up[:, half_of], dv, 1, 1, precision=HIGHEST)

    parts[10, 4:8] = jnp.zeros((4, 128), F32)
    parts[11:16] = jnp.zeros((5, 8, 128), F32)
    for u in range(2):
        da_here[u]()
        received_half(r4a.at[u], big_a, u)
        for s in range(4 * u, 4 * u + 4):
            through_gate(s, big_a, sa, va, 0)
    gd = weight_part(0)
    db_here()
    big_b[...] = r4b[...].astype(F32).reshape(1024, 128)
    for s in range(8):
        through_gate(s, big_b, sb, vb, 256)
    gd = gd + weight_part(1)
    parts[0] = gd[0:8]
    parts[1] = gd[8:16]

    f_me = y * 4 + x
    g_me = z * 2 + h

    def in_plane(offset):
        y2 = lax.rem(y + offset[0], NY)
        x2 = lax.rem(x + offset[1], NX)
        device = (4 * z + 2 * lax.rem(y2, 2) + h, x2 * 2 + lax.div(y2, 2))
        return device, y2 * 4 + x2

    def in_column(offset):
        z2 = lax.rem(z + offset[0], NZ)
        h2 = 1 - h if offset[1] else h
        return (4 * z2 + 2 * lax.rem(y, 2) + h2, q), z2 * 2 + h2

    def spread(step, offsets, where, src, own, dst, received):
        pltpu.make_async_copy(src(own), dst, redsem.at[step, 1]).start()
        for offset in offsets:
            if offset == (0, 0):
                continue
            device, other = where(offset)
            pltpu.make_async_remote_copy(
                src_ref=src(other),
                dst_ref=dst,
                send_sem=redsem.at[step, 0],
                recv_sem=redsem.at[step, 1],
                device_id=device,
                device_id_type=MESH,
            ).start()
        others = parts.at[0:15]
        pending.append(pltpu.make_async_copy(others, others, redsem.at[step, 0]).wait)
        return pltpu.make_async_copy(received, received, redsem.at[step, 1]).wait

    plane_here = spread(
        0, FAR_PLANE, in_plane, lambda f: parts.at[f], f_me, level1.at[f_me], level1
    )

    def pair_gradient(s):
        lanes = pl.ds(s * 128, 128)
        dzb = dot(wmat[...], dproj[:, lanes]) + dot(wg[...], dgp[:, lanes])
        dzh = dzb * gain1c[...]
        zh = zhat1[:, lanes]
        dz = inv1[:, lanes] * (
            dzh
            - jnp.mean(dzh, axis=0, keepdims=True)
            - zh * jnp.mean(dzh * zh, axis=0, keepdims=True)
        )
        cells = jnp.transpose(dz).astype(BF16)
        pig[s] = cells[0:64]
        pig[8 + s] = cells[64:128]

    for s in range(0, 3):
        pair_gradient(s)
    plane_here()
    level1[0] = jnp.sum(level1[...], axis=0)
    column_here = spread(
        1, FAR_COLUMN, in_column, lambda g: level1.at[0], g_me, level2.at[g_me], level2
    )
    for s in range(3, 8):
        pair_gradient(s)
    pig_away = pltpu.make_async_copy(pig, pig_out, outsem.at[1])
    pig_away.start()
    pending.append(pig_away.wait)
    column_here()
    level2[0] = jnp.sum(level2[...], axis=0)
    whole_here = spread(
        2, FAR_PLANE, in_plane, lambda f: level2.at[0], f_me, whole.at[f_me], whole
    )
    whole_here()
    finish()


def unpack(whole_in, update_in, pig_in, gdown, gup, gmag, update, pig, *scratch):
    (whole, update_here, pig_here, gup_here, gmag_here, insem, outsem) = scratch
    here = (whole, update_here, pig_here)
    loads = [
        pltpu.make_async_copy(src, dst, insem.at[n])
        for n, (src, dst) in enumerate(zip((whole_in, update_in, pig_in), here))
    ]
    for load in loads:
        load.start()
    stores = []

    def store(src, dst):
        stores.append(pltpu.make_async_copy(src, dst, outsem.at[len(stores)]))
        stores[-1].start()

    loads[0].wait()
    for n in range(2):
        store(whole.at[n], gdown.at[pl.ds(8 * n, 8)])
    for p in range(4):
        gup_here[:, p * 128 : (p + 1) * 128] = whole[2 + 2 * p : 4 + 2 * p].reshape(16, 128)
        gmag_here[:, p * 128 : (p + 1) * 128] = whole[10, p : p + 1]
    store(gup_here, gup)
    store(gmag_here, gmag)
    loads[1].wait()
    store(update_here, update)
    loads[2].wait()
    store(pig_here, pig)
    for copy in stores:
        copy.wait()


def on_device(
    pair,
    input_norm_gain,
    input_norm_bias,
    frozen_base_weight,
    adapter_down_factor,
    adapter_up_factor,
    magnitude,
    output_gate_weight,
    output_projection_weight,
    centre_norm_gain,
    centre_norm_bias,
    cotangent,
):
    hbm = pl.BlockSpec(memory_space=pltpu.HBM)
    cells = (CH, 1024)
    message = (CH, 8, 128)
    by_chip = (8, 16, 8, 128)
    message_halves = (2, CH, 4, 128)
    by_chip_halves = (2, 8, 16, 4, 128)
    operands = (
        pair,
        input_norm_gain.reshape(1, CH),
        input_norm_bias.reshape(1, CH),
        frozen_base_weight,
        adapter_down_factor.T,
        adapter_up_factor,
        magnitude.reshape(1, 4 * CH),
        output_gate_weight,
        output_projection_weight,
        centre_norm_gain.reshape(1, CH),
        centre_norm_bias.reshape(1, CH),
        cotangent,
    )
    block = jax.ShapeDtypeStruct(pair.shape, BF16)
    update, pig, whole = pl.pallas_call(
        kernel,
        out_shape=(block, block, jax.ShapeDtypeStruct((16, 8, 128), F32)),
        in_specs=[hbm] * 12,
        out_specs=(hbm, hbm, hbm),
        scratch_shapes=[pltpu.VMEM(a.shape, a.dtype) for a in operands]
        + [
            pltpu.VMEM(pair.shape, BF16),
            pltpu.VMEM(pair.shape, BF16),
            pltpu.VMEM(message_halves, BF16),
            pltpu.VMEM(message, BF16),
            pltpu.VMEM(by_chip_halves, BF16),
            pltpu.VMEM(by_chip, BF16),
            pltpu.VMEM(by_chip_halves, BF16),
            pltpu.VMEM(message_halves, BF16),
            pltpu.VMEM(message_halves, BF16),
            pltpu.VMEM(by_chip_halves, BF16),
            pltpu.VMEM(by_chip_halves, BF16),
            pltpu.VMEM(by_chip, BF16),
            pltpu.VMEM(message_halves, BF16),
            pltpu.VMEM(message, BF16),
            pltpu.VMEM((2, 128, TOKENS), BF16),
            pltpu.VMEM((16, 2, 16, TOKENS), BF16),
            pltpu.VMEM((16, 16, TOKENS), BF16),
            pltpu.VMEM((16, 16, TOKENS), BF16),
            pltpu.VMEM((1024, 128), F32),
            pltpu.VMEM((1024, 128), F32),
            pltpu.VMEM((16, 16, TOKENS), F32),
            pltpu.VMEM((16, 8, TOKENS), F32),
            pltpu.VMEM((16, 2, 16, TOKENS), F32),
            pltpu.VMEM(cells, F32),
            pltpu.VMEM(cells, F32),
            pltpu.VMEM(cells, F32),
            pltpu.VMEM(cells, F32),
            pltpu.VMEM(cells, F32),
            pltpu.VMEM((1, 1024), F32),
            pltpu.VMEM(cells, BF16),
            pltpu.VMEM(cells, F32),
            pltpu.VMEM(cells, F32),
            pltpu.VMEM(cells, BF16),
            pltpu.VMEM((4 * CH, 1024), BF16),
            pltpu.VMEM((CH, 4 * CH), F32),
            pltpu.VMEM((CH, 4 * CH), BF16),
            pltpu.VMEM((4 * CH, CH), BF16),
            pltpu.VMEM((CH, 128), F32),
            pltpu.VMEM((CH, 128), F32),
            pltpu.VMEM((CH, 128), F32),
            pltpu.VMEM((16, 8, 128), F32),
            pltpu.VMEM((16, 8, 128), F32),
            pltpu.VMEM((16, 8, 128), F32),
            pltpu.SemaphoreType.DMA((10,)),
            pltpu.SemaphoreType.DMA((10,)),
            pltpu.SemaphoreType.DMA((4,)),
            pltpu.SemaphoreType.DMA((3, 2)),
            pltpu.SemaphoreType.DMA((12,)),
            pltpu.SemaphoreType.DMA((2,)),
        ],
        compiler_params=pltpu.CompilerParams(
            collective_id=0, has_side_effects=True, vmem_limit_bytes=VMEM_GRANT
        ),
    )(*operands)
    gdown, gup, gmag, update, pig = pl.pallas_call(
        unpack,
        out_shape=(
            jax.ShapeDtypeStruct((16, CH), F32),
            jax.ShapeDtypeStruct((16, 4 * CH), F32),
            jax.ShapeDtypeStruct((1, 4 * CH), F32),
            block,
            block,
        ),
        in_specs=[hbm] * 3,
        out_specs=(hbm,) * 5,
        scratch_shapes=[
            pltpu.VMEM((16, 8, 128), F32),
            pltpu.VMEM(block.shape, BF16),
            pltpu.VMEM(block.shape, BF16),
            pltpu.VMEM((16, 4 * CH), F32),
            pltpu.VMEM((1, 4 * CH), F32),
            pltpu.SemaphoreType.DMA((3,)),
            pltpu.SemaphoreType.DMA((6,)),
        ],
        compiler_params=pltpu.CompilerParams(vmem_limit_bytes=VMEM_GRANT),
    )(whole, update, pig)
    return update, pig, gdown.T, gup, gmag.reshape(4 * CH)


def solution(mesh):
    cells = P("row", "col", None)
    placed = (cells,) + (P(),) * 10 + (cells,)
    return jax.shard_map(
        on_device,
        mesh=mesh,
        in_specs=placed,
        out_specs=(cells, cells, P(), P(), P()),
        check_vma=False,
    )
```

```python
import jax
import jax.numpy as jnp
from jax import lax
from jax.experimental import pallas as pl
from jax.experimental.pallas import tpu as pltpu
from jax.sharding import PartitionSpec as P

MESH = pl.DeviceIdType.MESH
F32 = jnp.float32
BF16 = jnp.bfloat16
NZ, NY, NX = 8, 4, 4
CH = 128
TOKENS = 512
VMEM_GRANT = 63 * 2**20
HIGHEST = lax.Precision.HIGHEST
FAR_Z = (4, 3, 5, 2, 6, 1, 7, 0)
FAR_PLANE = sorted(
    ((dy, dx) for dy in range(NY) for dx in range(NX)),
    key=lambda o: -(min(o[0], NY - o[0]) + min(o[1], NX - o[1])),
)
FAR_COLUMN = sorted(
    ((dz, dh) for dz in range(NZ) for dh in range(2)),
    key=lambda o: -(2 * min(o[0], NZ - o[0]) + o[1]),
)


def dot(a, b, ca=1, cb=0, precision=None):
    return lax.dot_general(
        a, b, (((ca,), (cb,)), ((), ())), precision=precision, preferred_element_type=F32
    )


def far_first(k, n):
    return n // 2 + (1 - 2 * lax.rem(k, 2)) * lax.div(k + 1, 2)


def pair_up(first, second):
    last = first.ndim - 1
    low = lax.broadcasted_iota(jnp.int32, first.shape, last) < 64
    return (
        jnp.where(low, first, pltpu.roll(second, 64, last)),
        jnp.where(low, pltpu.roll(first, 64, last), second),
    )


def half_rows(big, u):
    return big[...].reshape(CH, 8, 128)[:, 4 * u : 4 * u + 4, :].astype(BF16)


def column(row_ref):
    n = row_ref.shape[1]
    return jnp.transpose(jnp.broadcast_to(row_ref[...], (128, n)))


def kernel(*refs):
    operands, (update_out, pig_out, whole), scratch = refs[:12], refs[12:15], refs[15:]
    (
        pair,
        gain1,
        bias1,
        base,
        down_t,
        up,
        mag,
        wg,
        wo,
        gain2,
        bias2,
        cot,
        update,
        pig,
        s1a,
        s1b,
        r1a,
        r1b,
        s2,
        r2,
        s3,
        r3,
        s4a,
        s4b,
        r4a,
        r4b,
        amat,
        bmat,
        dbsend,
        dbrecv,
        big_a,
        big_b,
        mid,
        half,
        dbs,
        sa,
        va,
        sb,
        vb,
        zhat1,
        inv1,
        zbt,
        gate,
        cott,
        dgp,
        dxhat,
        xbt,
        dproj,
        vmat,
        wmat,
        wmat_t,
        gain1c,
        gain2c,
        bias2c,
        parts,
        level1,
        level2,
        ssem,
        rsem,
        sibsem,
        redsem,
        insem,
        outsem,
    ) = scratch
    local = (pair, gain1, bias1, base, down_t, up, mag, wg, wo, gain2, bias2, cot)
    row = lax.axis_index("row")
    q = lax.axis_index("col")
    m = lax.div(row, 2)
    h = lax.rem(row, 2)
    z = lax.div(m, 2)
    x = lax.div(q, 2)
    y = lax.rem(q, 2) * 2 + lax.rem(m, 2)
    me = m * 8 + q
    sibling = (m * 2 + 1 - h, q)

    def chip_at(dz, dy, dx):
        z2 = lax.rem(z + dz, NZ)
        y2 = lax.rem(y + dy, NY)
        x2 = lax.rem(x + dx, NX)
        return z2 * 2 + lax.rem(y2, 2), x2 * 2 + lax.div(y2, 2)

    z_rows = [4 * lax.rem(z + dz, NZ) + h for dz in FAR_Z]

    def plane(t):
        y2 = lax.rem(y + far_first(lax.div(t, 4), NY), NY)
        x2 = lax.rem(x + far_first(lax.rem(t, 4), NX), NX)
        return 2 * lax.rem(y2, 2), x2 * 2 + lax.div(y2, 2)

    def to_all(act):
        def over_plane(t, carry):
            parity, q2 = plane(t)
            for z_row in z_rows:
                act(z_row + parity, q2)
            return carry

        lax.fori_loop(0, 15, over_plane, 0)
        parity, q2 = plane(15)
        for z_row in z_rows[:-1]:
            act(z_row + parity, q2)

    loads = [
        pltpu.make_async_copy(operand, here, insem.at[n])
        for n, (operand, here) in enumerate(zip(operands, local))
    ]
    for load in loads:
        load.start()

    barrier = pltpu.get_barrier_semaphore()

    def greet(row2, q2):
        pl.semaphore_signal(barrier, inc=1, device_id=(row2, q2), device_id_type=MESH)

    to_all(greet)
    for z_row in z_rows:
        greet(z_row + 2 * lax.rem(y, 2) + 1 - 2 * h, q)

    for load in loads:
        load.wait()
    pending = []

    def finish():
        for wait in pending:
            wait()

    v = base[...] + dot(down_t[...], up[...], 0, 0, precision=HIGHEST)
    nrm = jnp.sqrt(jnp.sum(v * v, axis=0, keepdims=True) + 1e-06)
    scale = mag[...] / nrm
    vmat[...] = v
    w = (v * scale).astype(BF16)
    wmat[...] = w
    wmat_t[...] = jnp.transpose(w.astype(F32)).astype(BF16)
    wg_t = jnp.transpose(wg[...].astype(F32)).astype(BF16)
    gain1c[...] = column(gain1)
    bias1c = column(bias1)
    gain2c[...] = column(gain2)
    bias2c[...] = column(bias2)

    def project(s, zb, first, sig_ref, val_ref, big):
        lanes = pl.ds(s * 128, 128)
        proj = dot(wmat_t[first : first + 256], zb)
        sig = jax.nn.sigmoid(proj[0:128])
        sig_ref[:, lanes] = sig
        gated = sig * proj[128:256]
        val_ref[:, lanes] = gated * (1.0 - sig)
        big[pl.ds(s, CH, stride=8), :] = gated

    for s in range(8):
        lanes = pl.ds(s * 128, 128)
        zs = jnp.concatenate([pair[s], pair[8 + s]], axis=0).astype(F32)
        zs = jnp.transpose(zs)
        mean = jnp.mean(zs, axis=0, keepdims=True)
        centred = zs - mean
        inv = lax.rsqrt(jnp.mean(centred * centred, axis=0, keepdims=True) + 1e-05)
        zh = centred * inv
        zhat1[:, lanes] = zh
        inv1[:, lanes] = inv
        zb = (zh * gain1c[...] + bias1c).astype(BF16)
        zbt[:, lanes] = zb
        project(s, zb, 256, sb, vb, big_b)
    s1b[...] = big_b[...].reshape(CH, 8, 128).astype(BF16)

    pl.semaphore_wait(barrier, 127 + NZ)

    def exchange(step, src, dst_slot, received, others):
        own = pltpu.make_async_copy(src(m, q), dst_slot, rsem.at[step])
        own.start()

        def send(row2, q2):
            pltpu.make_async_remote_copy(
                src_ref=src(lax.div(row2, 2), q2),
                dst_ref=dst_slot,
                send_sem=ssem.at[step],
                recv_sem=rsem.at[step],
                device_id=(row2, q2),
                device_id_type=MESH,
            ).start()

        to_all(send)
        pending.append(pltpu.make_async_copy(others, others, ssem.at[step]).wait)
        return pltpu.make_async_copy(received, received, rsem.at[step]).wait

    def from_cells(step, sent, received):
        return exchange(
            step,
            lambda m2, q2: sent.at[m2 * 8 + q2],
            received.at[q, m],
            received,
            sent.at[0:127],
        )

    def from_owner(step, sent, received):
        return exchange(
            step,
            lambda m2, q2: sent.at[m2, q2],
            received.at[me],
            received,
            received.at[0:127],
        )

    b_here = from_cells(0, s1b, r1b)
    a_here = []
    for u in range(2):
        for s in range(4 * u, 4 * u + 4):
            project(s, zbt[:, pl.ds(s * 128, 128)], 0, sa, va, big_a)
        s1a[u] = half_rows(big_a, u)
        a_here.append(from_cells(1 + u, s1a.at[u], r1a.at[u]))

    for s in range(8):
        lanes = pl.ds(s * 128, 128)
        g = jax.nn.sigmoid(dot(wg_t, zbt[:, lanes]))
        gate[:, lanes] = g
        cs = jnp.concatenate([cot[s], cot[8 + s]], axis=0).astype(F32)
        cs = jnp.transpose(cs)
        cott[:, lanes] = cs
        dxh = dot(wo[...], (cs * g).astype(BF16)) * gain2c[...]
        dxhat[:, lanes] = dxh - jnp.mean(dxh, axis=0, keepdims=True)

    def assemble(received, target):
        rows = received.shape[2]
        for p in range(4):
            lanes = pl.ds(p * 128, 128)
            even, odd = pair_up(received[2 * p].astype(F32), received[2 * p + 1].astype(F32))
            target[:, 0:rows, lanes] = even
            target[:, rows : 2 * rows, lanes] = odd

    def dispatch(value, messages):
        rows = value.shape[1] // 2
        for p in range(4):
            block = value[:, :, p * 128 : (p + 1) * 128]
            first, second = pair_up(block[:, 0:rows, :], block[:, rows : 2 * rows, :])
            messages[:, 2 * p] = first.astype(BF16)
            messages[:, 2 * p + 1] = second.astype(BF16)

    def to_sibling(n, src, dst):
        copy = pltpu.make_async_remote_copy(
            src_ref=src,
            dst_ref=dst,
            send_sem=sibsem.at[2 * n],
            recv_sem=sibsem.at[2 * n + 1],
            device_id=sibling,
            device_id_type=MESH,
        )
        copy.start()
        return copy.wait

    b_here()
    assemble(r1b, mid)
    bmat[:, pl.ds(h, 1)] = mid[...].astype(BF16).reshape(16, 1, 16, TOKENS)
    b_whole = to_sibling(0, bmat.at[:, h], bmat.at[:, h])
    x_here = []
    for u in range(2):
        a_here[u]()
        assemble(r1a.at[u], half)
        amat[u] = half[...].reshape(128, TOKENS).astype(BF16)
        if u == 0:
            b_whole()
        ball = bmat[...].reshape(TOKENS, TOKENS)
        dispatch(dot(amat[u], ball, 1, 1).reshape(16, 8, TOKENS), s2.at[u])
        x_here.append(from_owner(3 + u, s2.at[u], r2.at[u]))

    wo_t = jnp.transpose(wo[...].astype(F32)).astype(BF16)

    def centre(s):
        lanes = pl.ds(s * 128, 128)
        xsl = big_a[pl.ds(s, CH, stride=8), :]
        mean = jnp.mean(xsl, axis=0, keepdims=True)
        centred = xsl - mean
        inv = lax.rsqrt(jnp.mean(centred * centred, axis=0, keepdims=True) + 1e-05)
        xhat = centred * inv
        xbt[:, lanes] = (xhat * gain2c[...] + bias2c[...]).astype(BF16)
        dxh = dxhat[:, lanes]
        dx = inv * (dxh - xhat * jnp.mean(dxh * xhat, axis=0, keepdims=True))
        big_b[pl.ds(s, CH, stride=8), :] = dx

    def output(s):
        lanes = pl.ds(s * 128, 128)
        outp = dot(wo_t, xbt[:, lanes])
        g = gate[:, lanes]
        up_cells = jnp.transpose(g * outp).astype(BF16)
        update[s] = up_cells[0:64]
        update[8 + s] = up_cells[64:128]
        dgp[:, lanes] = (cott[:, lanes] * outp * g * (1.0 - g)).astype(BF16)

    def received_half(received, big, u):
        big.reshape(CH, 8, 128)[:, 4 * u : 4 * u + 4, :] = received[...].astype(F32)

    dx_here = []
    for u in range(2):
        x_here[u]()
        received_half(r2.at[u], big_a, u)
        for s in range(4 * u, 4 * u + 4):
            centre(s)
        s3[u] = half_rows(big_b, u)
        dx_here.append(from_cells(5 + u, s3.at[u], r3.at[u]))
    for s in range(8):
        output(s)
    update_away = pltpu.make_async_copy(update, update_out, outsem.at[0])
    update_away.start()
    pending.append(update_away.wait)

    da_here = []
    for u in range(2):
        dx_here[u]()
        assemble(r3.at[u], half)
        dxm = half[...].reshape(128, TOKENS)
        db_part = dot(jnp.transpose(dxm).astype(BF16), amat[u]).reshape(16, 2, 16, TOKENS)
        if u == 0:
            dbs[...] = db_part
        else:
            dbs[...] += db_part
            dbsend[...] = dbs[:, pl.ds(1 - h, 1)].reshape(16, 16, TOKENS).astype(BF16)
            db_whole = to_sibling(1, dbsend, dbrecv)
        da = dot(dxm.astype(BF16), bmat[...].reshape(TOKENS, TOKENS))
        dispatch(da.reshape(16, 8, TOKENS), s4a.at[u])
        da_here.append(from_owner(7 + u, s4a.at[u], r4a.at[u]))
    db_whole()
    mid[...] = dbs[:, pl.ds(h, 1)].reshape(16, 16, TOKENS) + dbrecv[...].astype(F32)
    dispatch(mid[...], s4b)
    db_here = from_owner(9, s4b, r4b)

    def through_gate(s, big, sig_ref, val_ref, first):
        lanes = pl.ds(s * 128, 128)
        d = big[pl.ds(s, CH, stride=8), :]
        sig = sig_ref[:, lanes]
        dproj[first : first + 128, lanes] = (d * val_ref[:, lanes]).astype(BF16)
        dproj[first + 128 : first + 256, lanes] = (d * sig).astype(BF16)

    def weight_part(n):
        half_of = slice(n * 256, n * 256 + 256)
        dw = dot(zbt[...], dproj[half_of, :], 1, 1) * (1.0 / TOKENS)
        v = vmat[:, half_of]
        mg = mag[:, half_of]
        nrm = jnp.sqrt(jnp.sum(v * v, axis=0, keepdims=True) + 1e-06)
        p_sum = jnp.sum(dw * v, axis=0, keepdims=True)
        dv = dw * (mg / nrm) - v * (mg * p_sum / (nrm * nrm * nrm))
        gu = dot(down_t[...], dv, precision=HIGHEST)
        gm = p_sum / nrm
        for p in range(2):
            lanes = slice(p * 128, p * 128 + 128)
            parts[2 + 4 * n + 2 * p] = gu[0:8, lanes]
            parts[3 + 4 * n + 2 * p] = gu[8:16, lanes]
            parts[10, 2 * n + p : 2 * n + p + 1] = gm[:, lanes]
        return dot(up[:, half_of], dv, 1, 1, precision=HIGHEST)

    parts[10, 4:8] = jnp.zeros((4, 128), F32)
    parts[11:16] = jnp.zeros((5, 8, 128), F32)
    for u in range(2):
        da_here[u]()
        received_half(r4a.at[u], big_a, u)
        for s in range(4 * u, 4 * u + 4):
            through_gate(s, big_a, sa, va, 0)
    gd = weight_part(0)
    db_here()
    big_b[...] = r4b[...].astype(F32).reshape(1024, 128)
    for s in range(8):
        through_gate(s, big_b, sb, vb, 256)
    gd = gd + weight_part(1)
    parts[0] = gd[0:8]
    parts[1] = gd[8:16]

    f_me = y * 4 + x
    g_me = z * 2 + h

    def in_plane(offset):
        y2 = lax.rem(y + offset[0], NY)
        x2 = lax.rem(x + offset[1], NX)
        device = (4 * z + 2 * lax.rem(y2, 2) + h, x2 * 2 + lax.div(y2, 2))
        return device, y2 * 4 + x2

    def in_column(offset):
        z2 = lax.rem(z + offset[0], NZ)
        h2 = 1 - h if offset[1] else h
        return (4 * z2 + 2 * lax.rem(y, 2) + h2, q), z2 * 2 + h2

    def spread(step, offsets, where, src, own, dst, received):
        pltpu.make_async_copy(src(own), dst, redsem.at[step, 1]).start()
        for offset in offsets:
            if offset == (0, 0):
                continue
            device, other = where(offset)
            pltpu.make_async_remote_copy(
                src_ref=src(other),
                dst_ref=dst,
                send_sem=redsem.at[step, 0],
                recv_sem=redsem.at[step, 1],
                device_id=device,
                device_id_type=MESH,
            ).start()
        others = parts.at[0:15]
        pending.append(pltpu.make_async_copy(others, others, redsem.at[step, 0]).wait)
        return pltpu.make_async_copy(received, received, redsem.at[step, 1]).wait

    plane_here = spread(
        0, FAR_PLANE, in_plane, lambda f: parts.at[f], f_me, level1.at[f_me], level1
    )

    def pair_gradient(s):
        lanes = pl.ds(s * 128, 128)
        dzb = dot(wmat[...], dproj[:, lanes]) + dot(wg[...], dgp[:, lanes])
        dzh = dzb * gain1c[...]
        zh = zhat1[:, lanes]
        dz = inv1[:, lanes] * (
            dzh
            - jnp.mean(dzh, axis=0, keepdims=True)
            - zh * jnp.mean(dzh * zh, axis=0, keepdims=True)
        )
        cells = jnp.transpose(dz).astype(BF16)
        pig[s] = cells[0:64]
        pig[8 + s] = cells[64:128]

    for s in range(0, 3):
        pair_gradient(s)
    plane_here()
    level1[0] = jnp.sum(level1[...], axis=0)
    column_here = spread(
        1, FAR_COLUMN, in_column, lambda g: level1.at[0], g_me, level2.at[g_me], level2
    )
    for s in range(3, 8):
        pair_gradient(s)
    pig_away = pltpu.make_async_copy(pig, pig_out, outsem.at[1])
    pig_away.start()
    pending.append(pig_away.wait)
    column_here()
    level2[0] = jnp.sum(level2[...], axis=0)
    whole_here = spread(
        2, FAR_PLANE, in_plane, lambda f: level2.at[0], f_me, whole.at[f_me], whole
    )
    whole_here()
    finish()


def unpack(whole_in, update_in, pig_in, gdown, gup, gmag, update, pig, *scratch):
    (whole, update_here, pig_here, gup_here, gmag_here, insem, outsem) = scratch
    here = (whole, update_here, pig_here)
    loads = [
        pltpu.make_async_copy(src, dst, insem.at[n])
        for n, (src, dst) in enumerate(zip((whole_in, update_in, pig_in), here))
    ]
    for load in loads:
        load.start()
    stores = []

    def store(src, dst):
        stores.append(pltpu.make_async_copy(src, dst, outsem.at[len(stores)]))
        stores[-1].start()

    loads[0].wait()
    for n in range(2):
        store(whole.at[n], gdown.at[pl.ds(8 * n, 8)])
    for p in range(4):
        gup_here[:, p * 128 : (p + 1) * 128] = whole[2 + 2 * p : 4 + 2 * p].reshape(16, 128)
        gmag_here[:, p * 128 : (p + 1) * 128] = whole[10, p : p + 1]
    store(gup_here, gup)
    store(gmag_here, gmag)
    loads[1].wait()
    store(update_here, update)
    loads[2].wait()
    store(pig_here, pig)
    for copy in stores:
        copy.wait()


def on_device(
    pair,
    input_norm_gain,
    input_norm_bias,
    frozen_base_weight,
    adapter_down_factor,
    adapter_up_factor,
    magnitude,
    output_gate_weight,
    output_projection_weight,
    centre_norm_gain,
    centre_norm_bias,
    cotangent,
):
    hbm = pl.BlockSpec(memory_space=pltpu.HBM)
    cells = (CH, 1024)
    message = (CH, 8, 128)
    by_chip = (8, 16, 8, 128)
    message_halves = (2, CH, 4, 128)
    by_chip_halves = (2, 8, 16, 4, 128)
    operands = (
        pair,
        input_norm_gain.reshape(1, CH),
        input_norm_bias.reshape(1, CH),
        frozen_base_weight,
        adapter_down_factor.T,
        adapter_up_factor,
        magnitude.reshape(1, 4 * CH),
        output_gate_weight,
        output_projection_weight,
        centre_norm_gain.reshape(1, CH),
        centre_norm_bias.reshape(1, CH),
        cotangent,
    )
    block = jax.ShapeDtypeStruct(pair.shape, BF16)
    update, pig, whole = pl.pallas_call(
        kernel,
        out_shape=(block, block, jax.ShapeDtypeStruct((16, 8, 128), F32)),
        in_specs=[hbm] * 12,
        out_specs=(hbm, hbm, hbm),
        scratch_shapes=[pltpu.VMEM(a.shape, a.dtype) for a in operands]
        + [
            pltpu.VMEM(pair.shape, BF16),
            pltpu.VMEM(pair.shape, BF16),
            pltpu.VMEM(message_halves, BF16),
            pltpu.VMEM(message, BF16),
            pltpu.VMEM(by_chip_halves, BF16),
            pltpu.VMEM(by_chip, BF16),
            pltpu.VMEM((2, 16, 8, 4, 128), BF16),
            pltpu.VMEM(message_halves, BF16),
            pltpu.VMEM(message_halves, BF16),
            pltpu.VMEM(by_chip_halves, BF16),
            pltpu.VMEM((2, 16, 8, 4, 128), BF16),
            pltpu.VMEM((16, 8, 8, 128), BF16),
            pltpu.VMEM(message_halves, BF16),
            pltpu.VMEM(message, BF16),
            pltpu.VMEM((2, 128, TOKENS), BF16),
            pltpu.VMEM((16, 2, 16, TOKENS), BF16),
            pltpu.VMEM((16, 16, TOKENS), BF16),
            pltpu.VMEM((16, 16, TOKENS), BF16),
            pltpu.VMEM((1024, 128), F32),
            pltpu.VMEM((1024, 128), F32),
            pltpu.VMEM((16, 16, TOKENS), F32),
            pltpu.VMEM((16, 8, TOKENS), F32),
            pltpu.VMEM((16, 2, 16, TOKENS), F32),
            pltpu.VMEM(cells, F32),
            pltpu.VMEM(cells, F32),
            pltpu.VMEM(cells, F32),
            pltpu.VMEM(cells, F32),
            pltpu.VMEM(cells, F32),
            pltpu.VMEM((1, 1024), F32),
            pltpu.VMEM(cells, BF16),
            pltpu.VMEM(cells, F32),
            pltpu.VMEM(cells, F32),
            pltpu.VMEM(cells, BF16),
            pltpu.VMEM(cells, F32),
            pltpu.VMEM(cells, BF16),
            pltpu.VMEM((4 * CH, 1024), BF16),
            pltpu.VMEM((CH, 4 * CH), F32),
            pltpu.VMEM((CH, 4 * CH), BF16),
            pltpu.VMEM((4 * CH, CH), BF16),
            pltpu.VMEM((CH, 128), F32),
            pltpu.VMEM((CH, 128), F32),
            pltpu.VMEM((CH, 128), F32),
            pltpu.VMEM((16, 8, 128), F32),
            pltpu.VMEM((16, 8, 128), F32),
            pltpu.VMEM((16, 8, 128), F32),
            pltpu.SemaphoreType.DMA((10,)),
            pltpu.SemaphoreType.DMA((10,)),
            pltpu.SemaphoreType.DMA((4,)),
            pltpu.SemaphoreType.DMA((3, 2)),
            pltpu.SemaphoreType.DMA((12,)),
            pltpu.SemaphoreType.DMA((2,)),
        ],
        compiler_params=pltpu.CompilerParams(
            collective_id=0, has_side_effects=True, vmem_limit_bytes=VMEM_GRANT
        ),
    )(*operands)
    gdown, gup, gmag, update, pig = pl.pallas_call(
        unpack,
        out_shape=(
            jax.ShapeDtypeStruct((16, CH), F32),
            jax.ShapeDtypeStruct((16, 4 * CH), F32),
            jax.ShapeDtypeStruct((1, 4 * CH), F32),
            block,
            block,
        ),
        in_specs=[hbm] * 3,
        out_specs=(hbm,) * 5,
        scratch_shapes=[
            pltpu.VMEM((16, 8, 128), F32),
            pltpu.VMEM(block.shape, BF16),
            pltpu.VMEM(block.shape, BF16),
            pltpu.VMEM((16, 4 * CH), F32),
            pltpu.VMEM((1, 4 * CH), F32),
            pltpu.SemaphoreType.DMA((3,)),
            pltpu.SemaphoreType.DMA((6,)),
        ],
        compiler_params=pltpu.CompilerParams(vmem_limit_bytes=VMEM_GRANT),
    )(whole, update, pig)
    return update, pig, gdown.T, gup, gmag.reshape(4 * CH)


def solution(mesh):
    cells = P("row", "col", None)
    placed = (cells,) + (P(),) * 10 + (cells,)
    return jax.shard_map(
        on_device,
        mesh=mesh,
        in_specs=placed,
        out_specs=(cells, cells, P(), P(), P()),
        check_vma=False,
    )
```
